32 devices in a mesh: member: 2 (over x), gx: 16 (over z, y, core).
Axes of the slice: x: 2, y: 2, z: 4, core: 2. Of those that a mesh axis runs over, the one named last changes fastest.
Arguments:
- thermal_state: float32 [16, 1024, 1024], P('member', 'gx'), parts along dimension 0, may hold values from -6 to 6
- seawater_drift: float32 [4, 1024, 1024], P('member', 'gx'), parts along dimension 0, may hold values from -3 to 3
- sea_site_indicator: int32 [1024, 1024], P('gx'), may hold values 0 or 1
- chosen_tile_numbers: int32 [128], P(('member', 'gx')), parts along dimension 0, may hold values from 0 to 255, as said below
- chosen_floe_indicator: int32 [128, 4096], P(('member', 'gx')), parts along dimension 0, may hold values 0 or 1
- areal_fraction: float32 [128, 5, 4096], P(('member', 'gx')), parts along dimension 0, may hold values from 0 to 0.2
- thickness_amount: float32 [128, 5, 4096], P(('member', 'gx')), parts along dimension 0, may hold values from 0.1 to 1.5
- floe_motion: float32 [128, 2, 4096], P(('member', 'gx')), parts along dimension 0, may hold values from -3 to 3
- internal_traction: float32 [128, 3, 4096], P(('member', 'gx')), parts along dimension 0, may hold values from -6 to 6
- wind_traction: float32 [128, 2, 4096], P(('member', 'gx')), parts along dimension 0, may hold values from -3 to 3
Outputs:
- sea_warmth_later: float32 [16, 1024, 1024], P('member', 'gx'), parts along dimension 0
- topmost_drift_later: float32 [4, 1024, 1024], P('member', 'gx'), parts along dimension 0
- floe_drift_later: float32 [128, 2, 4096], P(('member', 'gx')), parts along dimension 0
- floe_traction_later: float32 [128, 3, 4096], P(('member', 'gx')), parts along dimension 0
- thickness_class_amount_later: float32 [128, 5, 4096], P(('member', 'gx')), parts along dimension 0
The draws below stay inside these ranges and needn't reach their ends.
There are 2 independent parts, one for each index of `member`. The reference program is written for one: setup_inputs(seed, part) draws one part's arguments, and reference() takes and returns one part's arrays. A program takes and returns all parts, laid end to end along the dimension named above; an argument that names none is the same for every part. Nothing has to cross between parts.
Inputs may be any that keep to these rules, and one draw needn't show every extreme that they name: `chosen_tile_numbers`: distinct block numbers, listed in no particular order; row q is owned by index q // 4 of gx. No tile column (block number // 16) holds more than 8 listed blocks, and some column holds exactly 8.
All inputs are finite; a program needn't handle non-finite values. No bound on the sum of `sea_site_indicator` or of `chosen_floe_indicator` on one device may be relied on, other than what follows from the above.
Results may differ from the reference program's by a relative error of at most 0.0017.
Values may be sent and summed in bfloat16 or wider, within the bound.
No kernel may reach another device: no remote copies, remote signals or barrier semaphores. Data moves between devices by JAX's collectives and lax.ppermute only.
A program may use at most 128 MiB of HBM per device.

```python
import jax
import jax.numpy as jnp
from jax import lax

BS = 64
MESH_HEIGHT = 1024
CATS = 5
SEA_DEPTHS = 8
BLK_DEV = 4
SUBCYCLES = 4
NICE = 64
MESH_WIDTH = 1024
N_GX = 16


def draw_chosen_tile_numbers(key, part):
    key = jax.random.fold_in(key, 11)
    column_count = NICE // BLK_DEV
    tiles_across = MESH_HEIGHT // BS
    key_order, key_shift, key_rank, key_deal = jax.random.split(key, 4)
    order = jax.random.permutation(key_order, column_count)
    order = ((order - order[0] + column_count // 2) % column_count).astype(jnp.int32)
    shifts = jax.random.randint(key_shift, (column_count // 2,), 0, BLK_DEV + 1)
    shifts = shifts.at[0].set(BLK_DEV)
    counts_perm = jnp.concatenate([BLK_DEV + shifts, BLK_DEV - shifts]).astype(jnp.int32)
    counts = jnp.zeros((column_count,), jnp.int32).at[order].set(counts_perm)
    rank_keys = jax.random.split(key_rank, column_count)
    ranks = jax.vmap(lambda single: jax.random.permutation(single, tiles_across))(rank_keys)
    chosen = ranks < counts[:, None]
    numbers = jnp.arange(column_count * tiles_across, dtype=jnp.int32).reshape(column_count, tiles_across)
    keyed = jnp.where(chosen, numbers, numbers + column_count * tiles_across).reshape(-1)
    listed = jnp.sort(keyed)[:NICE]
    target = jnp.sum((listed < column_count // 2 * tiles_across).astype(jnp.int32))
    dealing = jax.random.permutation(key_deal, NICE).astype(jnp.int32)
    positions = jnp.arange(NICE, dtype=jnp.int32)
    dealing = jnp.where(dealing == target, dealing[0], jnp.where(positions == 0, target, dealing))
    return jnp.take(listed, dealing).astype(jnp.int32)


def place_ends(entries, key, low, largest):
    longest = entries.shape.index(max(entries.shape))
    spots = []
    for shift in (0, 1):
        where = [jax.random.randint(jax.random.fold_in(key, axis), (), 0, length) for axis, length in enumerate(entries.shape)]
        where[longest] = (where[longest] + shift) % entries.shape[longest]
        spots.append(tuple(where))
    return entries.at[spots[0]].set(low).at[spots[1]].set(largest)


def shard_levels(key, dims, shards, smallest, top_value):
    gain = 1.0
    for position, parts in shards:
        draws = jax.random.uniform(jax.random.fold_in(jax.random.fold_in(key, 6), position), (parts,), jnp.float32, smallest / len(shards), top_value / len(shards))
        gain = gain * jnp.repeat(jnp.exp(draws), dims[position] // parts).reshape((-1,) + (1,) * (len(dims) - 1 - position))
    return gain


def bell_draw(stream_key, dims, scale, limit, pieces=(), kind=jnp.bfloat16):
    drawn = jax.random.normal(stream_key, dims, jnp.float32) * scale
    if len(pieces) > 0:
        drawn = shard_levels(stream_key, dims, pieces, -0.22, 0.18) * drawn
    return jnp.clip(drawn, min=-limit, max=limit).astype(kind)


def setup_inputs(seed: int = 0, part: int = 0) -> dict:
    key_list = jax.random.split(jax.random.key(seed), 11)
    part_keys = jax.random.split(jax.random.fold_in(key_list[10], part), 11)
    return {
        "thermal_state": bell_draw(part_keys[0], (SEA_DEPTHS, MESH_WIDTH, MESH_HEIGHT), 1.0, 6.0, ((1, 16),), jnp.float32),
        "seawater_drift": bell_draw(part_keys[1], (2, MESH_WIDTH, MESH_HEIGHT), 0.5, 3.0, ((1, 16),), jnp.float32),
        "sea_site_indicator": place_ends((jax.random.randint(key_list[2], (MESH_WIDTH, MESH_HEIGHT), 0, 10) < 9).astype(jnp.int32), jax.random.fold_in(key_list[2], 1), 0, 1),
        "chosen_tile_numbers": draw_chosen_tile_numbers(jax.random.fold_in(jax.random.fold_in(key_list[10], part), 71), part),
        "chosen_floe_indicator": place_ends((jax.random.randint(part_keys[4], (NICE, BS * BS), 0, 5) < 4).astype(jnp.int32), jax.random.fold_in(part_keys[4], 1), 0, 1),
        "areal_fraction": jnp.clip(0.2 * jax.random.uniform(part_keys[5], (NICE, CATS, BS * BS), jnp.float32) ** shard_levels(part_keys[5], (NICE, CATS, BS * BS), ((0, 16),), -0.2, 0.2), 0.0, 0.2),
        "thickness_amount": jnp.clip(0.1 + 1.4 * jax.random.uniform(part_keys[6], (NICE, CATS, BS * BS), jnp.float32) ** shard_levels(part_keys[6], (NICE, CATS, BS * BS), ((0, 16),), -0.2, 0.2), 0.1, 1.5),
        "floe_motion": bell_draw(part_keys[7], (NICE, 2, BS * BS), 0.5, 3.0, ((0, 16),), jnp.float32),
        "internal_traction": bell_draw(part_keys[8], (NICE, 3, BS * BS), 1.0, 6.0, ((0, 16),), jnp.float32),
        "wind_traction": bell_draw(part_keys[9], (NICE, 2, BS * BS), 0.5, 3.0, ((0, 16),), jnp.float32),
    }


step_evp = 1.0
damping = 1.0
drag_water = 1.0
coriolis = 0.5
strength_scale = 2.0
strength_decay = 5.0
ecc_square = 4.0
delta_floor = 0.1
growth_rate = 0.5
freezing = -1.8
sideways_spreading_coefficient = 0.2
depthwise_spreading_coefficient = 0.2
heat_gain = 1.0
stress_gain = 1.0

def to_grid(blocks, chosen_tile_numbers):
    tiles_across = MESH_HEIGHT // BS
    lead = blocks.shape[1:-1]
    lead_count = len(lead)
    full = jnp.zeros((N_GX * tiles_across,) + lead + (BS * BS,), blocks.dtype).at[chosen_tile_numbers].set(blocks)
    full = full.reshape((N_GX, tiles_across) + lead + (BS, BS))
    order = tuple(range(2, 2 + lead_count)) + (0, 2 + lead_count, 1, 3 + lead_count)
    return full.transpose(order).reshape(lead + (N_GX * BS, MESH_HEIGHT))

def from_grid(grid, chosen_tile_numbers):
    tiles_across = MESH_HEIGHT // BS
    lead = grid.shape[:-2]
    lead_count = len(lead)
    full = grid.reshape(lead + (N_GX, BS, tiles_across, BS))
    order = (lead_count, lead_count + 2) + tuple(range(lead_count)) + (lead_count + 1, lead_count + 3)
    full = full.transpose(order).reshape((N_GX * tiles_across,) + lead + (BS * BS,))
    return full[chosen_tile_numbers]

def to_east(field):
    return jnp.roll(field, -1, -2)

def to_west(field):
    return jnp.roll(field, 1, -2)

def to_north(field):
    return jnp.concatenate([field[..., 1:], jnp.zeros_like(field[..., :1])], -1)

def to_south(field):
    return jnp.concatenate([jnp.zeros_like(field[..., :1]), field[..., :-1]], -1)

def smoothing_contribution(field):
    return to_east(field) + to_west(field) + to_north(field) + to_south(field) - 4.0 * field

def reference(thermal_state, seawater_drift, sea_site_indicator, chosen_tile_numbers, chosen_floe_indicator, areal_fraction, thickness_amount, floe_motion, internal_traction, wind_traction):
    water_site_total = sea_site_indicator.astype(jnp.float32)
    joint_outcome = jnp.stack([thermal_state[0], seawater_drift[0], seawater_drift[1]]).astype(jnp.bfloat16)
    joint_outcome = lax.optimization_barrier(joint_outcome).astype(jnp.float32)
    sea_temp, ocean_u, ocean_v = (joint_outcome[0], joint_outcome[1], joint_outcome[2])
    ice_cells = to_grid(chosen_floe_indicator[:, None, :], chosen_tile_numbers)[0].astype(jnp.float32)
    conc_grid = to_grid(areal_fraction, chosen_tile_numbers)
    volume_grid = to_grid(thickness_amount, chosen_tile_numbers)
    ice_cover = lax.optimization_barrier(jnp.sum(conc_grid, 0))
    thickness = lax.optimization_barrier(jnp.sum(volume_grid, 0))
    strength = strength_scale * thickness * jnp.exp(-strength_decay * (1.0 - ice_cover))
    inertia = thickness / step_evp
    wind_grid = to_grid(wind_traction, chosen_tile_numbers)
    velocity_grid = to_grid(floe_motion, chosen_tile_numbers)
    stress_grid = to_grid(internal_traction, chosen_tile_numbers)
    ice_u, ice_v = (velocity_grid[0], velocity_grid[1])
    sigma_one, sigma_two, sigma_shear = (stress_grid[0], stress_grid[1], stress_grid[2])
    for subcycle in range(SUBCYCLES):
        normal_x = 0.5 * (sigma_one + sigma_two)
        normal_y = 0.5 * (sigma_one - sigma_two)
        force_x = 0.5 * (to_east(normal_x) - to_west(normal_x)) + 0.5 * (to_north(sigma_shear) - to_south(sigma_shear))
        force_y = 0.5 * (to_east(sigma_shear) - to_west(sigma_shear)) + 0.5 * (to_north(normal_y) - to_south(normal_y))
        denominator = inertia + drag_water
        new_u = (inertia * ice_u + force_x + wind_grid[0] + drag_water * ocean_u + coriolis * thickness * ice_v) / denominator * ice_cells
        new_v = (inertia * ice_v + force_y + wind_grid[1] + drag_water * ocean_v - coriolis * thickness * ice_u) / denominator * ice_cells
        ice_u, ice_v = (new_u, new_v)
        grad_ux = 0.5 * (to_east(ice_u) - to_west(ice_u))
        grad_vy = 0.5 * (to_north(ice_v) - to_south(ice_v))
        grad_uy = 0.5 * (to_north(ice_u) - to_south(ice_u))
        grad_vx = 0.5 * (to_east(ice_v) - to_west(ice_v))
        divergence = grad_ux + grad_vy
        tension = grad_ux - grad_vy
        shearing = grad_uy + grad_vx
        deform = jnp.sqrt(divergence * divergence + (tension * tension + shearing * shearing) / ecc_square + delta_floor * delta_floor)
        sigma_one = (sigma_one + damping * strength * (divergence / deform - 1.0)) / (1.0 + damping) * ice_cells
        sigma_two = (sigma_two + damping * strength * tension / (ecc_square * deform)) / (1.0 + damping) * ice_cells
        sigma_shear = (sigma_shear + damping * strength * shearing / (2.0 * ecc_square * deform)) / (1.0 + damping) * ice_cells
    heat_excess = sea_temp - freezing
    category_bias = 1.5 - 0.5 * jnp.arange(CATS, dtype=jnp.float32)
    growth = growth_rate * conc_grid * (category_bias[:, None, None] - heat_excess) / (1.0 + volume_grid) * ice_cells
    volume_updated = jnp.maximum(volume_grid + growth, 0.0)
    heat_flux = lax.optimization_barrier(jnp.sum(volume_updated - volume_grid, 0))
    tau_x = drag_water * ice_cover * (ice_u - ocean_u) * ice_cells
    tau_y = drag_water * ice_cover * (ice_v - ocean_v) * ice_cells
    fluxes = jnp.stack([heat_flux, tau_x, tau_y]).astype(jnp.bfloat16)
    fluxes = lax.optimization_barrier(fluxes).astype(jnp.float32)
    topmost_slab = thermal_state[1:] - thermal_state[:-1]
    vacant_slab = jnp.zeros_like(thermal_state[:1])
    depthwise_blending = jnp.concatenate([topmost_slab, vacant_slab], 0) - jnp.concatenate([vacant_slab, topmost_slab], 0)
    change_speed = sideways_spreading_coefficient * smoothing_contribution(thermal_state) + depthwise_spreading_coefficient * depthwise_blending
    change_speed = change_speed.at[0].add(heat_gain * fluxes[0])
    sea_warmth_later = thermal_state + water_site_total * change_speed
    topmost_drift_later = seawater_drift + water_site_total * (sideways_spreading_coefficient * smoothing_contribution(seawater_drift) + stress_gain * fluxes[1:])
    floe_drift_later = from_grid(jnp.stack([ice_u, ice_v]), chosen_tile_numbers)
    floe_traction_later = from_grid(jnp.stack([sigma_one, sigma_two, sigma_shear]), chosen_tile_numbers)
    thickness_class_amount_later = from_grid(volume_updated, chosen_tile_numbers)
    return (sea_warmth_later, topmost_drift_later, floe_drift_later, floe_traction_later, thickness_class_amount_later)
```

```python
import functools

import jax
import jax.numpy as jnp
import numpy as np
from jax import lax
from jax.experimental import pallas as pl
from jax.experimental.pallas import tpu as pltpu
from jax.sharding import PartitionSpec as P

BS = 64
SUBCYCLES = 4
KMAX = 8
M = 16
W = 8
NF = 9
ROWS1 = 176
ROWS2 = 128
ROWS3 = 32
ROWS4 = 48
RIM = 48
VMEM = 48 * 2**20
f32, bf16 = jnp.float32, jnp.bfloat16


def lanes(shape):
    return lax.broadcasted_iota(jnp.int32, shape, len(shape) - 1)


def roll(x, shift, axis=-1):
    axis = axis % x.ndim
    shift = shift % x.shape[axis]
    return x if shift == 0 else pltpu.roll(x, shift, axis)


def call(kernel, out_shape, scratch=(), in_specs=None, out_specs=None, **kw):
    return pl.pallas_call(
        kernel,
        out_shape=out_shape,
        in_specs=in_specs,
        out_specs=out_specs,
        scratch_shapes=list(scratch),
        compiler_params=pltpu.CompilerParams(vmem_limit_bytes=VMEM),
        **kw,
    )


def pack_kernel(ids, temp, drift, cells, conc, vol, motion, stress, wind, out, nat, rows, rim):
    tiles = temp.shape[2] // BS
    step = 512
    for start in range(0, BS * BS, step):
        sl = pl.ds(start, step)
        ice = cells[:, sl].astype(f32)
        cover = jnp.sum(conc[:, :, sl], axis=1)
        thick = jnp.sum(vol[:, :, sl], axis=1)
        nat[0, :, sl] = thick * ice
        nat[1, :, sl] = 2.0 * thick * jnp.exp(-5.0 * (1.0 - cover))
        nat[9, :, sl] = cover
        for k in range(2):
            nat[2 + k, :, sl] = wind[:, k, sl]
            nat[4 + k, :, sl] = motion[:, k, sl]
        for k in range(3):
            nat[6 + k, :, sl] = stress[:, k, sl]
    lane = lanes((4, 128))
    low, high = (lane & 63) < W, (lane & 63) >= BS - W
    which = lax.broadcasted_iota(jnp.int32, (4, 128), 0)
    listed = jnp.zeros((4, 128), f32)
    for q in range(4):
        number = ids[q]
        column, row = number // tiles, number % tiles
        pair = jnp.where(lane < 64, column, row).astype(f32)
        listed = jnp.where(which == q, pair, listed)
    rim[:, 36:40, :] = jnp.broadcast_to(listed[None], (M, 4, 128))
    rim[:, 40:48, :] = jnp.zeros((M, 8, 128), f32)
    for f in range(NF):
        at = slice(4 * f, 4 * f + 4)
        for k in range(4):
            rim[k, at, :] = nat[f, :, 128 * k : 128 * k + 128]
            rim[4 + k, at, :] = nat[f, :, 3584 + 128 * k : 3712 + 128 * k]
            first = jnp.zeros((4, 128), f32)
            last = jnp.zeros((4, 128), f32)
            for t in range(8):
                v = nat[f, :, 128 * (8 * k + t) : 128 * (8 * k + t) + 128]
                first = first + roll(jnp.where(low, v, 0.0), 8 * t)
                last = last + roll(jnp.where(high, v, 0.0), 8 * t)
            rim[8 + k, at, :] = first
            rim[12 + k, at, :] = last
    for m in range(M):
        start = (5 * m - W) % BS
        for k in range(2):
            left = min(5, BS - start)
            rows[5 * k : 5 * k + left, :] = drift[k, start : start + left, :]
            if left < 5:
                rows[5 * k + left : 5 * k + 5, :] = drift[k, 0 : 5 - left, :]
        rows[10:14, :] = temp[0, 4 * m : 4 * m + 4, :]
        rows[14:16, :] = jnp.zeros((2, rows.shape[1]), f32)
        tile = rows[...].astype(bf16)
        for part in range(8):
            out[m, 16 * part : 16 * part + 16, :] = tile[:, 128 * part : 128 * part + 128]
        out[m, 128:ROWS1, :] = rim[m].astype(bf16)


def route_kernel(count, me, got, everyone, table, out, s_sea, s_rim, row_of, acc):
    me_now = me[0]
    m = lax.rem(me_now, M)
    first = me_now - m
    east = m < 4
    west = jnp.logical_and(m >= 4, m < 8)
    north = jnp.logical_and(m >= 8, m < 12)
    shift_c = jnp.where(east, 1, jnp.where(west, -1, 0))
    shift_r = jnp.where(north, 1, jnp.where(m >= 12, -1, 0))
    lists = got[:, 160:176, :].reshape(M * 16, 128).astype(f32)
    number = lists[:, 0:1] * 16.0 + lists[:, 64:65]
    aim = table[0:1, :]
    hit = lax.broadcasted_iota(jnp.int32, (M * 16, M * RIM), 0) == aim
    number_lane = jnp.sum(jnp.where(hit, number, 0.0), axis=0, keepdims=True).astype(jnp.int32)
    code_one = jnp.where(aim >= 0, number_lane * 16 + table[1:2, :], -100)
    code_four = jnp.where(aim >= 0, number_lane * 16 + table[2:3, :], -100)
    lane = lanes((64, 128))
    part = lax.broadcasted_iota(jnp.int32, (64, 128), 0) >> 2

    def build(o, _):
        base = pl.multiple_of(o * 64, 64)
        here = everyone[o, everyone.shape[1] - 16 :, :]
        pick = lanes((64, 16)) == 4 + (lax.broadcasted_iota(jnp.int32, (64, 16), 0) & 3)
        both = jnp.dot(pick.astype(bf16), here, preferred_element_type=f32)
        other = roll(both, 64)
        column = jnp.where(lane < 64, both, other).astype(jnp.int32)
        row = jnp.where(lane < 64, other, both).astype(jnp.int32)
        row_of[pl.ds(base, 64), :] = row
        wide = 5 * m + jnp.where(part < 5, part, part - 5)
        delta = jnp.where(wide < W, -1, jnp.where(wide >= BS + W, 1, 0))
        delta = jnp.where(part >= 10, 0, delta)
        source = column + delta
        source = jnp.where(source < 0, source + count, source)
        source = jnp.where(source >= count, source - count, source) - first
        code = jnp.where((source >= 0) & (source < M) & (part < 14), source * 16 + part, -1)
        for k in range(2):
            s_sea[pl.ds(base, 64), 128 * k : 128 * k + 128] = (
                (lane + 128 * k) == code
            ).astype(bf16)
        tc = column + shift_c
        tc = jnp.where(tc < 0, tc + count, tc)
        tc = jnp.where(tc >= count, tc - count, tc)
        tr = row + shift_r
        one = jnp.where((tr >= 0) & (tr < 16) & (part < NF), (tc * 16 + tr) * 16 + part, -1)
        corner = (part >= NF) & (part < NF + 3)
        before = jnp.where(corner & (tr >= 1), (tc * 16 + tr - 1) * 16 + part - NF, -1)
        after = jnp.where(corner & (tr < 15), (tc * 16 + tr + 1) * 16 + part - NF, -1)
        span = M * RIM
        for k in range(span // 128):
            cut = slice(128 * k, 128 * k + 128)
            s_rim[pl.ds(base, 64), cut] = (code_one[:, cut] == one).astype(bf16)
            s_rim[pl.ds(base, 64), span + 128 * k : span + 128 * k + 128] = (
                code_four[:, cut] == before
            ).astype(bf16)
            s_rim[pl.ds(base, 64), 2 * span + 128 * k : 2 * span + 128 * k + 128] = (
                code_four[:, cut] == after
            ).astype(bf16)
        return 0

    lax.fori_loop(0, count, build, 0)

    rims = got[:, 128:ROWS1, :]
    wide_rims = rims.astype(f32)
    lane3 = lanes(wide_rims.shape)
    quarter = (lax.broadcasted_iota(jnp.int32, wide_rims.shape, 1) >> 2) & 3
    halves = []
    for mask in ((lane3 & 63) >= BS - W, (lane3 & 63) < W):
        kept = jnp.where(mask, wide_rims, 0.0)
        moved = kept
        for i in range(1, 4):
            moved = jnp.where(quarter == i, roll(kept, 16 * i), moved)
        halves.append(moved.astype(bf16).reshape(M * RIM, 128))
    span = M * RIM
    total = jnp.dot(s_rim[:, :span], rims.reshape(span, 128), preferred_element_type=f32)
    total = total + jnp.dot(s_rim[:, span : 2 * span], halves[0], preferred_element_type=f32)
    total = total + jnp.dot(s_rim[:, 2 * span :], halves[1], preferred_element_type=f32)
    out[:, 64:128, :] = total.astype(bf16).reshape(count, 64, 128)

    for k in range(8):
        sea = got[:, 16 * k : 16 * k + 16, :].reshape(M * 16, 128)
        value = jnp.dot(s_sea[...], sea, preferred_element_type=f32)
        place = 128 * k + lanes(value.shape) - row_of[...] * BS + W
        value = jnp.where((place >= 0) & (place < BS + 2 * W), value, 0.0)
        if k == 0:
            acc[...] = value
        else:
            acc[...] += value
    value = acc[...]
    value = jnp.where((row_of[...] & 1) == 1, roll(value, W + 64), roll(value, W))
    out[:, 0:64, :] = value.astype(bf16).reshape(count, 64, 128)


def ice_kernel(got, nat, conc, vol, motion, stress, grown, out, wide, ext, temp, flux):
    for m in range(M):
        wide[m] = got[m].astype(f32)
    lane = lanes((8, 128))
    lane4 = lanes((4, 128))

    def rim(m, j):
        return wide[m, 4 * j : 4 * j + 4, :]

    def two(a, b):
        return jnp.concatenate([a, b], axis=0)

    def natural(f, r):
        return two(
            nat[f, :, 128 * r : 128 * r + 128], nat[f, :, 128 * (r + 16) : 128 * (r + 16) + 128]
        )

    for f in range(11):
        ext[f, 0] = jnp.zeros((8, 128), f32)
        ext[f, 49] = jnp.zeros((8, 128), f32)
    for f in range(NF):
        for r in range(16):
            t = r % 8
            v = natural(f, r)
            north = two(rim(8 + r // 8, 16 + f), rim(10 + r // 8, 16 + f))
            south = two(rim(12 + r // 8, 16 + f), rim(14 + r // 8, 16 + f))
            for p in range(2):
                value = jnp.where(lane < 72, roll(v, 8 - 64 * p), roll(north, 72 - 64 * p - 8 * t))
                value = jnp.where(lane < 8, roll(south, -(56 + 64 * p + 8 * t)), value)
                ext[f, 1 + 8 + 2 * r + p] = value
        for y in range(8):
            p, i = y % 2, f % 4
            centre = two(rim(4 + y // 2, 16 + f), rim(y // 2, 16 + f))
            corner = two(
                rim(4 + y // 2, 16 + NF + f // 4), rim(y // 2, 16 + NF + f // 4)
            )
            value = jnp.where(
                lane < 72, roll(centre, 8 - 64 * p), roll(corner, 72 - 64 * p - 16 * i)
            )
            value = jnp.where(lane < 8, roll(corner, -(56 + 64 * p + 16 * i)), value)
            ext[f, 1 + y] = two(value[0:4], ext[f, 33 + y, 0:4, :])
            ext[f, 41 + y] = two(ext[f, 9 + y, 4:8, :], value[4:8])
    for y in range(48):
        for k in range(2):
            a, b = y, y + 32
            value = two(rim(a // 5, 5 * k + a % 5), rim(b // 5, 5 * k + b % 5))
            ext[9 + k, 1 + y] = value
            ext[2 + k, 1 + y] = ext[2 + k, 1 + y] + value
    thick = ext[0, 1:49]
    ext[11, 1:49] = jnp.where(thick > 0.0, 1.0 / (thick + 1.0), 0.0)
    ext[1, 1:49] = jnp.where(thick > 0.0, 0.5 * ext[1, 1:49], 0.0)

    step = 8

    def speed(i, _):
        at = pl.ds(1 + i * step, step)
        full = pl.ds(i * step, step + 2)
        one, two_, shear = ext[6, full], ext[7, full], ext[8, full]
        add = one + two_
        sub = one[1:-1] - two_[1:-1]
        mid = shear[1:-1]
        fx = 0.25 * (add[2:] - add[:-2]) + 0.5 * (roll(mid, -1) - roll(mid, 1))
        fy = 0.5 * (shear[2:] - shear[:-2]) + 0.25 * (roll(sub, -1) - roll(sub, 1))
        thick, inverse = ext[0, at], ext[11, at]
        u, v = ext[4, at], ext[5, at]
        half = 0.5 * thick
        ext[4, at] = (thick * u + fx + ext[2, at] + half * v) * inverse
        ext[5, at] = (thick * v + fy + ext[3, at] - half * u) * inverse
        return 0

    def strain(i, _):
        at = pl.ds(1 + i * step, step)
        full = pl.ds(i * step, step + 2)
        uu, vv = ext[4, full], ext[5, full]
        u, v = uu[1:-1], vv[1:-1]
        ux = uu[2:] - uu[:-2]
        vx = vv[2:] - vv[:-2]
        uy = roll(u, -1) - roll(u, 1)
        vy = roll(v, -1) - roll(v, 1)
        divergence = 0.5 * (ux + vy)
        tension = 0.5 * (ux - vy)
        shearing = 0.5 * (uy + vx)
        inverse = lax.rsqrt(
            divergence * divergence + 0.25 * (tension * tension + shearing * shearing) + 0.01
        )
        half = jnp.where(ext[0, at] > 0.0, 0.5, 0.0)
        strong = ext[1, at]
        scaled = strong * inverse
        ext[6, at] = half * ext[6, at] + (scaled * divergence - strong)
        ext[7, at] = half * ext[7, at] + 0.25 * scaled * tension
        ext[8, at] = half * ext[8, at] + 0.125 * scaled * shearing
        return 0

    for _ in range(SUBCYCLES):
        lax.fori_loop(0, 48 // step, speed, 0)
        lax.fori_loop(0, 48 // step, strain, 0)

    def flat(f, r):
        a, b = ext[f, 9 + 2 * r], ext[f, 10 + 2 * r]
        return jnp.where(lane < 64, roll(a, -8), roll(b, 56))

    for r in range(32):
        a, b = rim(r // 2, 10 + 2 * (r % 2)), rim(r // 2, 11 + 2 * (r % 2))
        temp[:, 128 * r : 128 * r + 128] = jnp.where(lane4 < 64, roll(a, -8), roll(b, 56))
    flux[:, 24:32, :] = jnp.zeros((M, 8, 128), f32)
    for r in range(16):
        for f in range(3):
            value = flat(6 + f, r)
            stress[:, f, 128 * r : 128 * r + 128] = value[0:4]
            stress[:, f, 128 * (r + 16) : 128 * (r + 16) + 128] = value[4:8]
        cover, ice = natural(9, r), natural(0, r) > 0.0
        for f in range(2):
            value = flat(4 + f, r)
            motion[:, f, 128 * r : 128 * r + 128] = value[0:4]
            motion[:, f, 128 * (r + 16) : 128 * (r + 16) + 128] = value[4:8]
            tau = jnp.where(ice, cover * (value - flat(9 + f, r)), 0.0)
            at = 4 * ((f + 1) * 2 + r % 2)
            flux[r // 2, at : at + 4, :] = tau[0:4]
            flux[8 + r // 2, at : at + 4, :] = tau[4:8]
    step = 512
    bias = 1.5 - 0.5 * lax.broadcasted_iota(jnp.int32, (conc.shape[1], step), 0).astype(f32)
    for q in range(4):
        for start in range(0, BS * BS, step):
            sl = pl.ds(start, step)
            volume = vol[q, :, sl]
            excess = temp[q : q + 1, sl] + 1.8
            ice = nat[0, q : q + 1, sl] > 0.0
            rate = 0.5 * conc[q, :, sl] * (bias - excess) / (1.0 + volume)
            later = jnp.maximum(volume + jnp.where(ice, rate, 0.0), 0.0)
            grown[q, :, sl] = later
            heat = jnp.sum(later - volume, axis=0, keepdims=True)
            for k in range(step // 128):
                r = start // 128 + k
                at = 4 * (r % 2) + q
                flux[r // 2, at : at + 1, :] = heat[:, 128 * k : 128 * k + 128]
    for m in range(M):
        out[m] = flux[m].astype(bf16)


def return_kernel(count, got, codes, out, pick):
    column = lax.broadcasted_iota(jnp.int32, (ROWS4, M * ROWS3), 0)
    local_code = (column & 7) * 8 + (column >> 3)
    span = codes[0:1, :]

    def build(c, _):
        base = pl.multiple_of(c * ROWS4, ROWS4)
        pick[pl.ds(base, ROWS4), :] = (span == local_code + c * 64).astype(bf16)
        return 0

    lax.fori_loop(0, count, build, 0)
    value = jnp.dot(pick[...], got[...].reshape(M * ROWS3, 128), preferred_element_type=f32)
    out[...] = value.astype(bf16).reshape(count, ROWS4, 128)


def ocean_kernel(temp, drift, wet, before, after, temp_out, drift_out):
    levels = temp.shape[0]
    shape = temp.shape[1:]
    lane = lanes(shape)
    row = lax.broadcasted_iota(jnp.int32, shape, 0)
    sea = wet[...].astype(f32)
    for k in range(levels + drift.shape[0]):
        mid = temp[k] if k < levels else drift[k - levels]
        east = jnp.where(row == shape[0] - 1, after[k], roll(mid, -1, 0))
        west = jnp.where(row == 0, before[k], roll(mid, 1, 0))
        north = jnp.where(lane == shape[1] - 1, 0.0, roll(mid, -1))
        south = jnp.where(lane == 0, 0.0, roll(mid, 1))
        change = 0.2 * (east + west + north + south - 4.0 * mid)
        if k < levels:
            vertical = jnp.zeros(shape, f32)
            if k + 1 < levels:
                vertical = vertical + (temp[k + 1] - mid)
            if k > 0:
                vertical = vertical - (mid - temp[k - 1])
            temp_out[k] = mid + sea * (change + 0.2 * vertical)
        else:
            drift_out[k - levels] = mid + sea * change


def final_kernel(rows, got, wet, temp, drift, temp_out, drift_out, wide, flux):
    for m in range(M):
        wide[pl.ds(ROWS4 * m, ROWS4), :] = got[m].astype(f32)
    flux[...] = jnp.zeros(flux.shape, f32)
    upper = lanes((M, 128)) >= 64
    for slot in range(KMAX):
        r = rows[slot]
        at = r // 2
        odd = lax.rem(r, 2) == 1
        keep = upper == odd
        for f in range(3):
            for h in range(2):
                value = wide[pl.ds(8 * (2 * f + h) + slot, M, stride=ROWS4), :]
                turned = roll(value, 64)
                for p in range(2):
                    chosen = jnp.where(odd, turned, value) if p == 0 else jnp.where(odd, value, turned)
                    to = (at, pl.ds(BS * f + 2 * h + p, M, stride=4), slice(None))
                    flux[to] = flux[to] + jnp.where(keep, chosen, 0.0)
    for part in range(flux.shape[0]):
        cut = slice(128 * part, 128 * part + 128)
        sea = wet[:, cut].astype(f32)
        temp_out[0, :, cut] = temp[0, :, cut] + sea * flux[part, 0:BS, :]
        for k in range(2):
            added = sea * flux[part, BS * (k + 1) : BS * (k + 2), :]
            drift_out[k, :, cut] = drift[k, :, cut] + added


def local(
    thermal_state,
    seawater_drift,
    sea_site_indicator,
    chosen_tile_numbers,
    chosen_floe_indicator,
    areal_fraction,
    thickness_amount,
    floe_motion,
    internal_traction,
    wind_traction,
):
    count = lax.axis_size("gx")
    groups = count // M
    me = lax.axis_index("gx")
    tiles = thermal_state.shape[2] // BS
    members = [[g * M + i for i in range(M)] for g in range(groups)]
    smem = pl.BlockSpec(memory_space=pltpu.SMEM)
    vmem = pl.BlockSpec(memory_space=pltpu.VMEM)
    depth, height = thermal_state.shape[1:]
    top = pl.BlockSpec((1, depth, height), lambda i: (0, 0, 0))

    def whole(x):
        return pl.BlockSpec(x.shape, lambda i, n=len(x.shape): (0,) * n)

    def within(x):
        if groups == 1:
            return lax.all_to_all(x, "gx", 0, 0, tiled=True)
        return lax.all_to_all(x, "gx", 0, 0, axis_index_groups=members, tiled=True)

    def across(x):
        x = lax.all_to_all(x, "gx", 0, 0, tiled=True)
        if groups == 1:
            return x
        return jnp.sum(x.reshape((groups, M) + x.shape[1:]).astype(f32), 0).astype(bf16)

    tail = jnp.concatenate([thermal_state[:, depth - 1 :], seawater_drift[:, depth - 1 :]], 0)
    head = jnp.concatenate([thermal_state[:, :1], seawater_drift[:, :1]], 0)
    before = lax.ppermute(tail, "gx", [(i, (i + 1) % count) for i in range(count)])
    after = lax.ppermute(head, "gx", [((i + 1) % count, i) for i in range(count)])

    arrays = (
        thermal_state,
        seawater_drift,
        chosen_floe_indicator,
        areal_fraction,
        thickness_amount,
        floe_motion,
        internal_traction,
        wind_traction,
    )
    nat_shape = jax.ShapeDtypeStruct((10, 4, BS * BS), f32)
    one_shape = jax.ShapeDtypeStruct((M, ROWS1, 128), bf16)
    payload, nat = call(
        pack_kernel,
        (one_shape, nat_shape),
        scratch=(pltpu.VMEM((16, height), f32), pltpu.VMEM((M, RIM, 128), f32)),
        grid=(1,),
        in_specs=[smem, top] + [whole(x) for x in arrays[1:]],
        out_specs=(whole(one_shape), whole(nat_shape)),
    )(chosen_tile_numbers, *arrays)
    got1 = within(payload)

    index = np.arange(M * RIM)
    source, place = index // RIM, index % RIM
    table = np.zeros((8, M * RIM), np.int32)
    table[0] = np.where(place < 4 * NF, source * 16 + 4 + place % 4, -1)
    table[1] = place // 4
    table[2] = place // 16
    if groups == 1:
        everyone = got1
    else:
        mine = payload[0, 160:176]
        everyone = lax.all_gather(mine, "gx", axis=0, tiled=False)
    payload2 = call(
        functools.partial(route_kernel, count),
        jax.ShapeDtypeStruct((count, ROWS2, 128), bf16),
        scratch=(
            pltpu.VMEM((count * 64, M * 16), bf16),
            pltpu.VMEM((count * 64, 3 * M * RIM), bf16),
            pltpu.VMEM((count * 64, 128), jnp.int32),
            pltpu.VMEM((count * 64, 128), f32),
        ),
        in_specs=[smem, vmem, vmem, vmem],
        out_specs=vmem,
    )(me.reshape(1).astype(jnp.int32), got1, everyone, jnp.asarray(table))
    got2 = across(payload2)

    pairs = everyone[:, everyone.shape[1] - 12 : everyone.shape[1] - 8, :].astype(f32)
    columns = pairs[:, :, 0].reshape(-1).astype(jnp.int32)
    rows = pairs[:, :, 64].reshape(-1).astype(jnp.int32)
    ranks = jnp.sum(
        ((columns[None, :] == columns[:, None]) & (rows[None, :] < rows[:, None])).astype(jnp.int32), 1
    )
    slot = jnp.arange(KMAX, dtype=jnp.int32)
    mine = (columns[None, :] == me) & (ranks[None, :] == slot[:, None])
    slot_rows = jnp.sum(jnp.where(mine, rows[None, :], 0), 1)
    code = columns * 64 + ranks * 8
    code = lax.dynamic_slice_in_dim(code, (me // M) * (M * 4), M * 4, 0)
    item = jnp.arange(8, dtype=jnp.int32)
    codes = code.reshape(M, 1, 4) + item[None, :, None]
    codes = jnp.where(item[None, :, None] < 6, codes, -1).reshape(1, M * ROWS3)

    temp_new, drift_new = call(
        ocean_kernel,
        (
            jax.ShapeDtypeStruct(thermal_state.shape, f32),
            jax.ShapeDtypeStruct(seawater_drift.shape, f32),
        ),
        in_specs=[vmem] * 5,
        out_specs=(vmem, vmem),
        cost_estimate=pl.CostEstimate(flops=10**7, bytes_accessed=6 * 10**6, transcendentals=0),
    )(thermal_state, seawater_drift, sea_site_indicator, before, after)

    motion, stress, grown, payload3 = call(
        ice_kernel,
        (
            jax.ShapeDtypeStruct(floe_motion.shape, f32),
            jax.ShapeDtypeStruct(internal_traction.shape, f32),
            jax.ShapeDtypeStruct(thickness_amount.shape, f32),
            jax.ShapeDtypeStruct((M, ROWS3, 128), bf16),
        ),
        scratch=(
            pltpu.VMEM((M, ROWS2, 128), f32),
            pltpu.VMEM((12, 50, 8, 128), f32),
            pltpu.VMEM((4, BS * BS), f32),
            pltpu.VMEM((M, ROWS3, 128), f32),
        ),
        in_specs=[vmem] * 4,
        out_specs=(vmem,) * 4,
    )(got2, nat, areal_fraction, thickness_amount)
    got3 = within(payload3)

    payload4 = call(
        functools.partial(return_kernel, count),
        jax.ShapeDtypeStruct((count, ROWS4, 128), bf16),
        scratch=(pltpu.VMEM((count * ROWS4, M * ROWS3), bf16),),
        in_specs=[vmem, vmem],
        out_specs=vmem,
    )(got3, codes)
    got4 = across(payload4)

    temp_later, drift_later = call(
        final_kernel,
        (
            jax.ShapeDtypeStruct(thermal_state.shape, f32),
            jax.ShapeDtypeStruct(seawater_drift.shape, f32),
        ),
        scratch=(pltpu.VMEM((M * ROWS4, 128), f32), pltpu.VMEM((height // 128, 3 * BS, 128), f32)),
        grid=(1,),
        in_specs=[smem, whole(got4), whole(sea_site_indicator), top, whole(drift_new)],
        out_specs=(top, whole(drift_new)),
        input_output_aliases={3: 0, 4: 1},
    )(slot_rows, got4, sea_site_indicator, temp_new, drift_new)
    return temp_later, drift_later, motion, stress, grown


def solution(mesh):
    return jax.shard_map(
        local,
        mesh=mesh,
        in_specs=(
            P("member", "gx", None),
            P("member", "gx", None),
            P("gx", None),
            P(("member", "gx")),
            P(("member", "gx"), None),
            P(("member", "gx"), None, None),
            P(("member", "gx"), None, None),
            P(("member", "gx"), None, None),
            P(("member", "gx"), None, None),
            P(("member", "gx"), None, None),
        ),
        out_specs=(
            P("member", "gx", None),
            P("member", "gx", None),
            P(("member", "gx"), None, None),
            P(("member", "gx"), None, None),
            P(("member", "gx"), None, None),
        ),
        check_vma=False,
    )
```

```python
import functools

import jax
import jax.numpy as jnp
from jax import lax
from jax.experimental import pallas as pl
from jax.experimental.pallas import tpu as pltpu
from jax.sharding import PartitionSpec as P

BS = 64
SUBCYCLES = 4
KMAX = 8
M = 16
W = 8
NF = 9
ROWS1 = 160
ROWS2 = 96
ROWS3 = 32
ROWS4 = 48
VMEM = 60 * 2**20
ROOM = 40 * 2**20
f32, bf16 = jnp.float32, jnp.bfloat16


def lanes(shape):
    return lax.broadcasted_iota(jnp.int32, shape, len(shape) - 1)


def roll(x, shift, axis=-1):
    axis = axis % x.ndim
    shift = shift % x.shape[axis]
    return x if shift == 0 else pltpu.roll(x, shift, axis)


def call(kernel, out_shape, scratch=(), in_specs=None, out_specs=None, vmem=VMEM, **kw):
    return pl.pallas_call(
        kernel,
        out_shape=out_shape,
        in_specs=in_specs,
        out_specs=out_specs,
        scratch_shapes=list(scratch),
        compiler_params=pltpu.CompilerParams(vmem_limit_bytes=vmem),
        **kw,
    )


def pack_kernel(ids, temp, drift, cells, conc, vol, motion, stress, wind, out, nat, big):
    tiles = temp.shape[2] // BS
    step = 512
    for start in range(0, BS * BS, step):
        sl = pl.ds(start, step)
        ice = cells[:, sl].astype(f32)
        cover = jnp.sum(conc[:, :, sl], axis=0)
        thick = jnp.sum(vol[:, :, sl], axis=0)
        nat[0, :, sl] = thick * ice
        nat[1, :, sl] = 2.0 * thick * jnp.exp(-5.0 * (1.0 - cover))
        nat[9, :, sl] = cover
        for k in range(2):
            nat[2 + k, :, sl] = wind[:, k, sl]
            nat[4 + k, :, sl] = motion[:, k, sl]
        for k in range(3):
            nat[6 + k, :, sl] = stress[k, :, sl]
    lane = lanes((4, 128))
    low, high = (lane & 63) < W, (lane & 63) >= BS - W
    lane_all = lanes((12, 128))
    row_all = lax.broadcasted_iota(jnp.int32, (12, 128), 0)
    listed = jnp.zeros((12, 128), f32)
    for q in range(4):
        number = ids[q]
        column, row = number // tiles, number % tiles
        listed = jnp.where(lane_all == q, column.astype(f32), listed)
        listed = jnp.where(lane_all == 4 + q, row.astype(f32), listed)
    listed = jnp.where(row_all == 0, listed, 0.0)
    for m in range(M):
        big[m, 148:160, :] = listed
        start = (5 * m - W) % BS
        left = min(5, BS - start)
        for part in range(8):
            cut = slice(128 * part, 128 * part + 128)
            at = 14 * part
            for k in range(2):
                big[m, at + 5 * k : at + 5 * k + left, :] = drift[k, start : start + left, cut]
                if left < 5:
                    big[m, at + 5 * k + left : at + 5 * k + 5, :] = drift[k, 0 : 5 - left, cut]
            big[m, at + 10 : at + 14, :] = temp[0, 4 * m : 4 * m + 4, cut]
    for f in range(NF):
        at = slice(112 + 4 * f, 116 + 4 * f)
        for k in range(4):
            big[k, at, :] = nat[f, :, 128 * k : 128 * k + 128]
            big[4 + k, at, :] = nat[f, :, 3584 + 128 * k : 3712 + 128 * k]
            first = jnp.zeros((4, 128), f32)
            last = jnp.zeros((4, 128), f32)
            for t in range(8):
                v = nat[f, :, 128 * (8 * k + t) : 128 * (8 * k + t) + 128]
                first = first + roll(jnp.where(low, v, 0.0), 8 * t)
                last = last + roll(jnp.where(high, v, 0.0), 8 * t)
            big[8 + k, at, :] = first
            big[12 + k, at, :] = last
    for m in range(M):
        out[m] = big[m].astype(bf16)


def route_kernel(count, me, got, everyone, out, wide, sea, listed, numbers, collect, sem):
    listed[...] = everyone[:, everyone.shape[1] - 16 :, :].astype(f32)[:, 4, :].astype(jnp.int32)
    copy = pltpu.make_async_copy(listed, numbers, sem)
    copy.start()
    me_now = me[0]
    m = lax.rem(me_now, M)
    first = me_now - m
    for s in range(M):
        wide[s] = got[s].astype(f32)
        for part in range(8):
            sea[s, part, 0:14, :] = wide[s, 14 * part : 14 * part + 14, :]

    east = m < 4
    west = jnp.logical_and(m >= 4, m < 8)
    north = jnp.logical_and(m >= 8, m < 12)
    shift_c = jnp.where(east, 1, jnp.where(west, -1, 0))
    shift_r = jnp.where(north, 1, jnp.where(m >= 12, -1, 0))
    size = count * 4

    def by_row(values, owners):
        n = owners * 4
        spread = jnp.broadcast_to(values[:, None, :], (owners, 4, 128)).reshape(n, 128)
        q = lax.broadcasted_iota(jnp.int32, (n, 128), 0) & 3
        lane = lanes((n, 128))
        column = jnp.sum(jnp.where(lane == q, spread, 0.0), axis=1, keepdims=True)
        row = jnp.sum(jnp.where(lane == q + 4, spread, 0.0), axis=1, keepdims=True)
        return column, row

    column, row = by_row(listed[...].astype(f32), count)
    own = wide[:, 148, :]
    own_column, own_row = by_row(own, M)
    own_number = own_column * 16.0 + own_row
    eye = lax.broadcasted_iota(jnp.int32, (64, 64), 0) == lanes((64, 64))
    number = jnp.sum(jnp.where(eye, own_number, 0.0), axis=0, keepdims=True)
    tc = column + shift_c.astype(f32)
    tc = jnp.where(tc < 0, tc + count, tc)
    tc = jnp.where(tc >= count, tc - count, tc)
    tr = row + shift_r.astype(f32)

    def one_hot(r):
        code = jnp.where((r >= 0) & (r < 16), tc * 16.0 + r, -1.0)
        return (code == number).astype(bf16)

    centre = one_hot(tr)
    before = one_hot(jnp.where(tr >= 0, tr - 1.0, -1.0))
    after = one_hot(jnp.where(tr < 16, tr + 1.0, 16.0))
    lane = lanes((64, 128))
    low, high = (lane & 63) < W, (lane & 63) >= BS - W
    for jj in range(3):
        first_part = jnp.zeros((64, 128), f32)
        last_part = jnp.zeros((64, 128), f32)
        for i in range(min(4, NF - 4 * jj)):
            f = 4 * jj + i
            field = wide[:, 112 + 4 * f : 116 + 4 * f, :].reshape(64, 128)
            value = jnp.dot(centre, field.astype(bf16), preferred_element_type=f32)
            collect[:, 60 + 4 * f : 64 + 4 * f, :] = value.reshape(count, 4, 128)
            last_part = last_part + roll(jnp.where(high, field, 0.0), 16 * i)
            first_part = first_part + roll(jnp.where(low, field, 0.0), 16 * i)
        value = jnp.dot(before, last_part.astype(bf16), preferred_element_type=f32)
        value = value + jnp.dot(after, first_part.astype(bf16), preferred_element_type=f32)
        collect[:, 48 + 4 * jj : 52 + 4 * jj, :] = value.reshape(count, 4, 128)

    copy.wait()
    lane = lanes((10, 128))
    k = lax.broadcasted_iota(jnp.int32, (10, 128), 0)
    wide_row = 5 * m + jnp.where(k < 5, k, k - 5)
    beside = jnp.where(wide_row < W, 1, jnp.where(wide_row >= BS + W, 1, 0)) == 1
    step = jnp.where(m < 8, -1, 1)
    lane2 = lanes((1, 128))

    def cut(o, _):
        for q in range(4):
            c, r = numbers[o, q], numbers[o, 4 + q]
            other = c + step
            other = jnp.where(other < 0, other + count, jnp.where(other >= count, other - count, other))
            c, other = c - first, other - first
            c_in = jnp.logical_and(c >= 0, c < M).astype(jnp.int32)
            o_in = jnp.logical_and(other >= 0, other < M).astype(jnp.int32)
            c, other = jnp.clip(c, 0, M - 1), jnp.clip(other, 0, M - 1)
            half, odd = r >> 1, r & 1
            near = half + 2 * odd - 1
            near_in = jnp.logical_and(near >= 0, near < 8).astype(jnp.int32)
            near = jnp.clip(near, 0, 7)
            a = jnp.where(beside, sea[other, half, 0:10, :], sea[c, half, 0:10, :])
            b = jnp.where(beside, sea[other, near, 0:10, :], sea[c, near, 0:10, :])
            inside = jnp.where(odd == 1, (lane >= 56).astype(jnp.int32), (lane < 72).astype(jnp.int32))
            edge = jnp.where(odd == 1, (lane < W).astype(jnp.int32), (lane >= 128 - W).astype(jnp.int32))
            known = jnp.where(beside, o_in, c_in)
            value = jnp.where(inside * known == 1, a, jnp.where(edge * near_in * known == 1, b, 0.0))
            collect[o, pl.ds(q, 10, stride=4), :] = pltpu.roll(value, W + 64 * odd, 1)
            warm = sea[c, half, 10:14, :] * c_in.astype(f32)
            turn = pltpu.roll(warm, 64, 1)
            straight = jnp.where(odd == 1, turn, warm)
            crossed = jnp.where(odd == 1, warm, turn)
            for i in range(2):
                pair = jnp.where(lane2 < 64, straight[2 * i : 2 * i + 1], crossed[2 * i + 1 : 2 * i + 2])
                collect[o, 40 + 4 * i + q : 41 + 4 * i + q, :] = pair
        return 0

    lax.fori_loop(0, count, cut, 0)
    for o in range(count):
        out[o] = collect[o].astype(bf16)


def ice_kernel(got, nat, conc, vol, motion, stress, grown, out, wide, ext, temp, flux):
    for m in range(M):
        wide[m] = got[m].astype(f32)
    lane = lanes((8, 128))

    def rim(m, j):
        return wide[m, 4 * j : 4 * j + 4, :]

    def two(a, b):
        return jnp.concatenate([a, b], axis=0)

    def natural(f, r):
        return two(
            nat[f, :, 128 * r : 128 * r + 128], nat[f, :, 128 * (r + 16) : 128 * (r + 16) + 128]
        )

    for f in range(11):
        ext[f, 0] = jnp.zeros((8, 128), f32)
        ext[f, 49] = jnp.zeros((8, 128), f32)
    for f in range(NF):
        for r in range(16):
            t = r % 8
            v = natural(f, r)
            north = two(rim(8 + r // 8, 15 + f), rim(10 + r // 8, 15 + f))
            south = two(rim(12 + r // 8, 15 + f), rim(14 + r // 8, 15 + f))
            for p in range(2):
                value = jnp.where(lane < 72, roll(v, 8 - 64 * p), roll(north, 72 - 64 * p - 8 * t))
                value = jnp.where(lane < 8, roll(south, -(56 + 64 * p + 8 * t)), value)
                ext[f, 1 + 8 + 2 * r + p] = value
        for y in range(8):
            p, i = y % 2, f % 4
            centre = two(rim(4 + y // 2, 15 + f), rim(y // 2, 15 + f))
            corner = two(
                rim(4 + y // 2, 12 + f // 4), rim(y // 2, 12 + f // 4)
            )
            value = jnp.where(
                lane < 72, roll(centre, 8 - 64 * p), roll(corner, 72 - 64 * p - 16 * i)
            )
            value = jnp.where(lane < 8, roll(corner, -(56 + 64 * p + 16 * i)), value)
            ext[f, 1 + y] = two(value[0:4], ext[f, 33 + y, 0:4, :])
            ext[f, 41 + y] = two(ext[f, 9 + y, 4:8, :], value[4:8])
    for y in range(48):
        for k in range(2):
            a, b = y, y + 32
            value = two(rim(a // 5, 5 * k + a % 5), rim(b // 5, 5 * k + b % 5))
            ext[9 + k, 1 + y] = value
            ext[2 + k, 1 + y] = ext[2 + k, 1 + y] + value
    thick = ext[0, 1:49]
    ext[11, 1:49] = jnp.where(thick > 0.0, 1.0 / (thick + 1.0), 0.0)
    ext[1, 1:49] = jnp.where(thick > 0.0, 0.5 * ext[1, 1:49], 0.0)

    step = 8

    def speed(i, _):
        at = pl.ds(1 + i * step, step)
        full = pl.ds(i * step, step + 2)
        one, two_, shear = ext[6, full], ext[7, full], ext[8, full]
        add = one + two_
        sub = one[1:-1] - two_[1:-1]
        mid = shear[1:-1]
        fx = 0.25 * (add[2:] - add[:-2]) + 0.5 * (roll(mid, -1) - roll(mid, 1))
        fy = 0.5 * (shear[2:] - shear[:-2]) + 0.25 * (roll(sub, -1) - roll(sub, 1))
        thick, inverse = ext[0, at], ext[11, at]
        u, v = ext[4, at], ext[5, at]
        half = 0.5 * thick
        ext[4, at] = (thick * u + fx + ext[2, at] + half * v) * inverse
        ext[5, at] = (thick * v + fy + ext[3, at] - half * u) * inverse
        return 0

    def strain(i, _):
        at = pl.ds(1 + i * step, step)
        full = pl.ds(i * step, step + 2)
        uu, vv = ext[4, full], ext[5, full]
        u, v = uu[1:-1], vv[1:-1]
        ux = uu[2:] - uu[:-2]
        vx = vv[2:] - vv[:-2]
        uy = roll(u, -1) - roll(u, 1)
        vy = roll(v, -1) - roll(v, 1)
        divergence = 0.5 * (ux + vy)
        tension = 0.5 * (ux - vy)
        shearing = 0.5 * (uy + vx)
        inverse = lax.rsqrt(
            divergence * divergence + 0.25 * (tension * tension + shearing * shearing) + 0.01
        )
        half = jnp.where(ext[0, at] > 0.0, 0.5, 0.0)
        strong = ext[1, at]
        scaled = strong * inverse
        ext[6, at] = half * ext[6, at] + (scaled * divergence - strong)
        ext[7, at] = half * ext[7, at] + 0.25 * scaled * tension
        ext[8, at] = half * ext[8, at] + 0.125 * scaled * shearing
        return 0

    for _ in range(SUBCYCLES):
        for i in range(48 // step):
            speed(i, 0)
        for i in range(48 // step):
            strain(i, 0)

    def flat(f, r):
        a, b = ext[f, 9 + 2 * r], ext[f, 10 + 2 * r]
        return jnp.where(lane < 64, roll(a, -8), roll(b, 56))

    for r in range(32):
        temp[:, 128 * r : 128 * r + 128] = rim(r // 2, 10 + r % 2)
    flux[:, 24:32, :] = jnp.zeros((M, 8, 128), f32)
    for r in range(16):
        for f in range(3):
            value = flat(6 + f, r)
            stress[f, :, 128 * r : 128 * r + 128] = value[0:4]
            stress[f, :, 128 * (r + 16) : 128 * (r + 16) + 128] = value[4:8]
        cover, ice = natural(9, r), natural(0, r) > 0.0
        for f in range(2):
            value = flat(4 + f, r)
            motion[:, f, 128 * r : 128 * r + 128] = value[0:4]
            motion[:, f, 128 * (r + 16) : 128 * (r + 16) + 128] = value[4:8]
            tau = jnp.where(ice, cover * (value - flat(9 + f, r)), 0.0)
            at = 4 * ((f + 1) * 2 + r % 2)
            flux[r // 2, at : at + 4, :] = tau[0:4]
            flux[8 + r // 2, at : at + 4, :] = tau[4:8]
    step = 512
    for start in range(0, BS * BS, step):
        sl = pl.ds(start, step)
        excess = temp[:, sl] + 1.8
        half = jnp.where(nat[0, :, sl] > 0.0, 0.5, 0.0)
        heat = jnp.zeros((4, step), f32)
        for n in range(conc.shape[0]):
            volume = vol[n, :, sl]
            rate = half * conc[n, :, sl] * ((1.5 - 0.5 * n) - excess) / (1.0 + volume)
            later = jnp.maximum(volume + rate, 0.0)
            grown[n, :, sl] = later
            heat = heat + (later - volume)
        for k in range(step // 128):
            r = start // 128 + k
            at = 4 * (r % 2)
            flux[r // 2, at : at + 4, :] = heat[:, 128 * k : 128 * k + 128]
    for m in range(M):
        out[m] = flux[m].astype(bf16)


def return_kernel(count, got, codes, out, pick):
    column = lax.broadcasted_iota(jnp.int32, (ROWS4, M * ROWS3), 0)
    local_code = (column & 7) * 8 + (column >> 3)
    span = codes[0:1, :]

    def build(c, _):
        base = pl.multiple_of(c * ROWS4, ROWS4)
        pick[pl.ds(base, ROWS4), :] = (span == local_code + c * 64).astype(bf16)
        return 0

    lax.fori_loop(0, count, build, 0)
    value = jnp.dot(pick[...], got[...].reshape(M * ROWS3, 128), preferred_element_type=f32)
    out[...] = value.astype(bf16).reshape(count, ROWS4, 128)


def ocean_kernel(temp, drift, wet, before, after, temp_out, drift_out):
    levels = temp.shape[0]
    shape = temp.shape[1:]
    lane = lanes(shape)
    row = lax.broadcasted_iota(jnp.int32, shape, 0)
    sea = wet[...].astype(f32)
    for k in range(levels + drift.shape[0]):
        mid = temp[k] if k < levels else drift[k - levels]
        east = jnp.where(row == shape[0] - 1, after[k], roll(mid, -1, 0))
        west = jnp.where(row == 0, before[k], roll(mid, 1, 0))
        north = jnp.where(lane == shape[1] - 1, 0.0, roll(mid, -1))
        south = jnp.where(lane == 0, 0.0, roll(mid, 1))
        change = 0.2 * (east + west + north + south - 4.0 * mid)
        if k < levels:
            vertical = jnp.zeros(shape, f32)
            if k + 1 < levels:
                vertical = vertical + (temp[k + 1] - mid)
            if k > 0:
                vertical = vertical - (mid - temp[k - 1])
            temp_out[k] = mid + sea * (change + 0.2 * vertical)
        else:
            drift_out[k - levels] = mid + sea * change


def final_kernel(rows, got, wet, temp, drift, temp_out, drift_out, wide, flux):
    for m in range(M):
        wide[pl.ds(ROWS4 * m, ROWS4), :] = got[m].astype(f32)
    flux[...] = jnp.zeros(flux.shape, f32)
    upper = lanes((M, 128)) >= 64
    for slot in range(KMAX):
        r = rows[slot]
        at = r // 2
        odd = lax.rem(r, 2) == 1
        keep = upper == odd
        for f in range(3):
            for h in range(2):
                value = wide[pl.ds(8 * (2 * f + h) + slot, M, stride=ROWS4), :]
                turned = roll(value, 64)
                for p in range(2):
                    chosen = jnp.where(odd, turned, value) if p == 0 else jnp.where(odd, value, turned)
                    to = (at, pl.ds(BS * f + 2 * h + p, M, stride=4), slice(None))
                    flux[to] = flux[to] + jnp.where(keep, chosen, 0.0)
    for part in range(flux.shape[0]):
        cut = slice(128 * part, 128 * part + 128)
        sea = wet[:, cut].astype(f32)
        temp_out[0, :, cut] = temp[0, :, cut] + sea * flux[part, 0:BS, :]
        for k in range(2):
            added = sea * flux[part, BS * (k + 1) : BS * (k + 2), :]
            drift_out[k, :, cut] = drift[k, :, cut] + added


def local(
    thermal_state,
    seawater_drift,
    sea_site_indicator,
    chosen_tile_numbers,
    chosen_floe_indicator,
    areal_fraction,
    thickness_amount,
    floe_motion,
    internal_traction,
    wind_traction,
):
    count = lax.axis_size("gx")
    groups = count // M
    me = lax.axis_index("gx")
    tiles = thermal_state.shape[2] // BS
    members = [[g * M + i for i in range(M)] for g in range(groups)]
    smem = pl.BlockSpec(memory_space=pltpu.SMEM)
    vmem = pl.BlockSpec(memory_space=pltpu.VMEM)
    depth, height = thermal_state.shape[1:]
    top = pl.BlockSpec((1, depth, height), lambda i: (0, 0, 0))

    def whole(x):
        return pl.BlockSpec(x.shape, lambda i, n=len(x.shape): (0,) * n)

    def within(x):
        if groups == 1:
            return lax.all_to_all(x, "gx", 0, 0, tiled=True)
        return lax.all_to_all(x, "gx", 0, 0, axis_index_groups=members, tiled=True)

    def across(x):
        x = lax.all_to_all(x, "gx", 0, 0, tiled=True)
        if groups == 1:
            return x
        return jnp.sum(x.reshape((groups, M) + x.shape[1:]).astype(f32), 0).astype(bf16)

    tail = jnp.concatenate([thermal_state[:, depth - 1 :], seawater_drift[:, depth - 1 :]], 0)
    head = jnp.concatenate([thermal_state[:, :1], seawater_drift[:, :1]], 0)
    before = lax.ppermute(tail, "gx", [(i, (i + 1) % count) for i in range(count)])
    after = lax.ppermute(head, "gx", [((i + 1) % count, i) for i in range(count)])

    conc = jnp.transpose(areal_fraction, (1, 0, 2))
    vol = jnp.transpose(thickness_amount, (1, 0, 2))
    arrays = (
        thermal_state,
        seawater_drift,
        chosen_floe_indicator,
        conc,
        vol,
        floe_motion,
        jnp.transpose(internal_traction, (1, 0, 2)),
        wind_traction,
    )
    nat_shape = jax.ShapeDtypeStruct((10, 4, BS * BS), f32)
    one_shape = jax.ShapeDtypeStruct((M, ROWS1, 128), bf16)
    payload, nat = call(
        pack_kernel,
        (one_shape, nat_shape),
        scratch=(pltpu.VMEM((M, ROWS1, 128), f32),),
        grid=(1,),
        in_specs=[smem, top] + [whole(x) for x in arrays[1:]],
        out_specs=(whole(one_shape), whole(nat_shape)),
    )(chosen_tile_numbers, *arrays)
    got1 = within(payload)

    if groups == 1:
        everyone = got1
    else:
        mine = payload[0, 144:160]
        everyone = lax.all_gather(mine, "gx", axis=0, tiled=False)
    payload2 = call(
        functools.partial(route_kernel, count),
        jax.ShapeDtypeStruct((count, ROWS2, 128), bf16),
        scratch=(
            pltpu.VMEM((M, ROWS1, 128), f32),
            pltpu.VMEM((M, 8, 16, 128), f32),
            pltpu.VMEM((count, 128), jnp.int32),
            pltpu.SMEM((count, 128), jnp.int32),
            pltpu.VMEM((count, ROWS2, 128), f32),
            pltpu.SemaphoreType.DMA,
        ),
        in_specs=[smem, vmem, vmem],
        out_specs=vmem,
        vmem=ROOM,
    )(me.reshape(1).astype(jnp.int32), got1, everyone)
    got2 = across(payload2)

    pairs = everyone[:, everyone.shape[1] - 12, 0:8].astype(jnp.int32)
    columns, rows = pairs[:, :4].reshape(-1), pairs[:, 4:].reshape(-1)
    ranks = jnp.sum(
        ((columns[None, :] == columns[:, None]) & (rows[None, :] < rows[:, None])).astype(jnp.int32), 1
    )
    slot = jnp.arange(KMAX, dtype=jnp.int32)
    mine = (columns[None, :] == me) & (ranks[None, :] == slot[:, None])
    slot_rows = jnp.sum(jnp.where(mine, rows[None, :], 0), 1)
    code = columns * 64 + ranks * 8
    code = lax.dynamic_slice_in_dim(code, (me // M) * (M * 4), M * 4, 0)
    item = jnp.arange(8, dtype=jnp.int32)
    codes = code.reshape(M, 1, 4) + item[None, :, None]
    codes = jnp.where(item[None, :, None] < 6, codes, -1).reshape(1, M * ROWS3)

    temp_new, drift_new = call(
        ocean_kernel,
        (
            jax.ShapeDtypeStruct(thermal_state.shape, f32),
            jax.ShapeDtypeStruct(seawater_drift.shape, f32),
        ),
        in_specs=[vmem] * 5,
        out_specs=(vmem, vmem),
        cost_estimate=pl.CostEstimate(flops=10**7, bytes_accessed=6 * 10**6, transcendentals=0),
    )(thermal_state, seawater_drift, sea_site_indicator, before, after)

    motion, stress, grown, payload3 = call(
        ice_kernel,
        (
            jax.ShapeDtypeStruct(floe_motion.shape, f32),
            jax.ShapeDtypeStruct(arrays[6].shape, f32),
            jax.ShapeDtypeStruct(vol.shape, f32),
            jax.ShapeDtypeStruct((M, ROWS3, 128), bf16),
        ),
        scratch=(
            pltpu.VMEM((M, ROWS2, 128), f32),
            pltpu.VMEM((12, 50, 8, 128), f32),
            pltpu.VMEM((4, BS * BS), f32),
            pltpu.VMEM((M, ROWS3, 128), f32),
        ),
        in_specs=[vmem] * 4,
        out_specs=(vmem,) * 4,
        vmem=ROOM,
    )(got2, nat, conc, vol)
    stress = jnp.transpose(stress, (1, 0, 2))
    grown = jnp.transpose(grown, (1, 0, 2))
    got3 = within(payload3)

    payload4 = call(
        functools.partial(return_kernel, count),
        jax.ShapeDtypeStruct((count, ROWS4, 128), bf16),
        scratch=(pltpu.VMEM((count * ROWS4, M * ROWS3), bf16),),
        in_specs=[vmem, vmem],
        out_specs=vmem,
        vmem=ROOM,
    )(got3, codes)
    got4 = across(payload4)

    temp_later, drift_later = call(
        final_kernel,
        (
            jax.ShapeDtypeStruct(thermal_state.shape, f32),
            jax.ShapeDtypeStruct(seawater_drift.shape, f32),
        ),
        scratch=(pltpu.VMEM((M * ROWS4, 128), f32), pltpu.VMEM((height // 128, 3 * BS, 128), f32)),
        grid=(1,),
        in_specs=[smem, whole(got4), whole(sea_site_indicator), top, whole(drift_new)],
        out_specs=(top, whole(drift_new)),
        input_output_aliases={3: 0, 4: 1},
        vmem=ROOM,
    )(slot_rows, got4, sea_site_indicator, temp_new, drift_new)
    return temp_later, drift_later, motion, stress, grown


def solution(mesh):
    return jax.shard_map(
        local,
        mesh=mesh,
        in_specs=(
            P("member", "gx", None),
            P("member", "gx", None),
            P("gx", None),
            P(("member", "gx")),
            P(("member", "gx"), None),
            P(("member", "gx"), None, None),
            P(("member", "gx"), None, None),
            P(("member", "gx"), None, None),
            P(("member", "gx"), None, None),
            P(("member", "gx"), None, None),
        ),
        out_specs=(
            P("member", "gx", None),
            P("member", "gx", None),
            P(("member", "gx"), None, None),
            P(("member", "gx"), None, None),
            P(("member", "gx"), None, None),
        ),
        check_vma=False,
    )
```

```python
import functools

import jax
import jax.numpy as jnp
from jax import lax
from jax.experimental import pallas as pl
from jax.experimental.pallas import tpu as pltpu
from jax.sharding import PartitionSpec as P

BS = 64
SUBCYCLES = 4
KMAX = 8
M = 16
W = 8
NF = 9
ROWS1 = 152
ROWS2 = 96
ROWS3 = 24
ROWS4 = 48
VMEM = 60 * 2**20
ROOM = 40 * 2**20
f32, bf16 = jnp.float32, jnp.bfloat16


def lanes(shape):
    return lax.broadcasted_iota(jnp.int32, shape, len(shape) - 1)


def roll(x, shift, axis=-1):
    axis = axis % x.ndim
    shift = shift % x.shape[axis]
    return x if shift == 0 else pltpu.roll(x, shift, axis)


def call(kernel, out_shape, scratch=(), in_specs=None, out_specs=None, vmem=VMEM, **kw):
    return pl.pallas_call(
        kernel,
        out_shape=out_shape,
        in_specs=in_specs,
        out_specs=out_specs,
        scratch_shapes=list(scratch),
        compiler_params=pltpu.CompilerParams(vmem_limit_bytes=vmem),
        **kw,
    )


def pack_kernel(ids, temp, drift, cells, conc, vol, motion, stress, wind, out, nat, big):
    tiles = temp.shape[2] // BS
    step = 512
    for start in range(0, BS * BS, step):
        sl = pl.ds(start, step)
        ice = cells[:, sl].astype(f32)
        cover = jnp.sum(conc[:, :, sl], axis=0)
        thick = jnp.sum(vol[:, :, sl], axis=0)
        nat[0, :, sl] = thick * ice
        nat[1, :, sl] = 2.0 * thick * jnp.exp(-5.0 * (1.0 - cover))
        nat[9, :, sl] = cover
        for k in range(2):
            nat[2 + k, :, sl] = wind[:, k, sl]
            nat[4 + k, :, sl] = motion[:, k, sl]
        for k in range(3):
            nat[6 + k, :, sl] = stress[k, :, sl]
    lane = lanes((4, 128))
    low, high = (lane & 63) < W, (lane & 63) >= BS - W
    lane_all = lanes((4, 128))
    row_all = lax.broadcasted_iota(jnp.int32, (4, 128), 0)
    listed = jnp.zeros((4, 128), f32)
    for q in range(4):
        number = ids[q]
        column, row = number // tiles, number % tiles
        listed = jnp.where(lane_all == q, column.astype(f32), listed)
        listed = jnp.where(lane_all == 4 + q, row.astype(f32), listed)
    listed = jnp.where(row_all == 0, listed, 0.0)
    for m in range(M):
        big[m, 148:152, :] = listed
        start = (5 * m - W) % BS
        left = min(5, BS - start)
        for part in range(8):
            cut = slice(128 * part, 128 * part + 128)
            at = 14 * part
            for k in range(2):
                big[m, at + 5 * k : at + 5 * k + left, :] = drift[k, start : start + left, cut]
                if left < 5:
                    big[m, at + 5 * k + left : at + 5 * k + 5, :] = drift[k, 0 : 5 - left, cut]
            big[m, at + 10 : at + 14, :] = temp[0, 4 * m : 4 * m + 4, cut]
    for f in range(NF):
        at = slice(112 + 4 * f, 116 + 4 * f)
        for k in range(4):
            big[k, at, :] = nat[f, :, 128 * k : 128 * k + 128]
            big[4 + k, at, :] = nat[f, :, 3584 + 128 * k : 3712 + 128 * k]
            first = jnp.zeros((4, 128), f32)
            last = jnp.zeros((4, 128), f32)
            for t in range(8):
                v = nat[f, :, 128 * (8 * k + t) : 128 * (8 * k + t) + 128]
                first = first + roll(jnp.where(low, v, 0.0), 8 * t)
                last = last + roll(jnp.where(high, v, 0.0), 8 * t)
            big[8 + k, at, :] = first
            big[12 + k, at, :] = last
    for m in range(M):
        out[m] = big[m].astype(bf16)


def route_kernel(count, me, got, everyone, out, wide, sea, listed, numbers, collect, sem):
    for s in range(M):
        wide[s] = got[s].astype(f32)
    if count == M:
        listed[...] = wide[:, 148, :].astype(jnp.int32)
    else:
        listed[...] = everyone[...].astype(f32)[:, 4, :].astype(jnp.int32)
    copy = pltpu.make_async_copy(listed, numbers, sem)
    copy.start()
    me_now = me[0]
    m = lax.rem(me_now, M)
    first = me_now - m
    for s in range(M):
        for part in range(8):
            sea[s, part, 0:14, :] = wide[s, 14 * part : 14 * part + 14, :]

    east = m < 4
    west = jnp.logical_and(m >= 4, m < 8)
    north = jnp.logical_and(m >= 8, m < 12)
    shift_c = jnp.where(east, 1, jnp.where(west, -1, 0))
    shift_r = jnp.where(north, 1, jnp.where(m >= 12, -1, 0))
    size = count * 4

    def by_row(values, owners):
        n = owners * 4
        spread = jnp.broadcast_to(values[:, None, :], (owners, 4, 128)).reshape(n, 128)
        q = lax.broadcasted_iota(jnp.int32, (n, 128), 0) & 3
        lane = lanes((n, 128))
        column = jnp.sum(jnp.where(lane == q, spread, 0.0), axis=1, keepdims=True)
        row = jnp.sum(jnp.where(lane == q + 4, spread, 0.0), axis=1, keepdims=True)
        return column, row

    column, row = by_row(listed[...].astype(f32), count)
    own = wide[:, 148, :]
    own_column, own_row = by_row(own, M)
    own_number = own_column * 16.0 + own_row
    eye = lax.broadcasted_iota(jnp.int32, (64, 64), 0) == lanes((64, 64))
    number = jnp.sum(jnp.where(eye, own_number, 0.0), axis=0, keepdims=True)
    tc = column + shift_c.astype(f32)
    tc = jnp.where(tc < 0, tc + count, tc)
    tc = jnp.where(tc >= count, tc - count, tc)
    tr = row + shift_r.astype(f32)

    def one_hot(r):
        code = jnp.where((r >= 0) & (r < 16), tc * 16.0 + r, -1.0)
        return (code == number).astype(bf16)

    centre = one_hot(tr)
    before = one_hot(jnp.where(tr >= 0, tr - 1.0, -1.0))
    after = one_hot(jnp.where(tr < 16, tr + 1.0, 16.0))
    lane = lanes((64, 128))
    low, high = (lane & 63) < W, (lane & 63) >= BS - W
    for jj in range(3):
        first_part = jnp.zeros((64, 128), f32)
        last_part = jnp.zeros((64, 128), f32)
        for i in range(min(4, NF - 4 * jj)):
            f = 4 * jj + i
            field = wide[:, 112 + 4 * f : 116 + 4 * f, :].reshape(64, 128)
            value = jnp.dot(centre, field.astype(bf16), preferred_element_type=f32)
            collect[:, 60 + 4 * f : 64 + 4 * f, :] = value.reshape(count, 4, 128)
            last_part = last_part + roll(jnp.where(high, field, 0.0), 16 * i)
            first_part = first_part + roll(jnp.where(low, field, 0.0), 16 * i)
        value = jnp.dot(before, last_part.astype(bf16), preferred_element_type=f32)
        value = value + jnp.dot(after, first_part.astype(bf16), preferred_element_type=f32)
        collect[:, 48 + 4 * jj : 52 + 4 * jj, :] = value.reshape(count, 4, 128)

    copy.wait()
    lane = lanes((10, 128))
    k = lax.broadcasted_iota(jnp.int32, (10, 128), 0)
    wide_row = 5 * m + jnp.where(k < 5, k, k - 5)
    beside = jnp.where(wide_row < W, 1, jnp.where(wide_row >= BS + W, 1, 0)) == 1
    step = jnp.where(m < 8, -1, 1)
    lane2 = lanes((1, 128))

    def cut(o, _):
        for q in range(4):
            c, r = numbers[o, q], numbers[o, 4 + q]
            other = c + step
            other = jnp.where(other < 0, other + count, jnp.where(other >= count, other - count, other))
            c, other = c - first, other - first
            c_in = jnp.logical_and(c >= 0, c < M).astype(jnp.int32)
            o_in = jnp.logical_and(other >= 0, other < M).astype(jnp.int32)
            c, other = jnp.clip(c, 0, M - 1), jnp.clip(other, 0, M - 1)
            half, odd = r >> 1, r & 1
            near = half + 2 * odd - 1
            near_in = jnp.logical_and(near >= 0, near < 8).astype(jnp.int32)
            near = jnp.clip(near, 0, 7)
            a = jnp.where(beside, sea[other, half, 0:10, :], sea[c, half, 0:10, :])
            b = jnp.where(beside, sea[other, near, 0:10, :], sea[c, near, 0:10, :])
            inside = jnp.where(odd == 1, (lane >= 56).astype(jnp.int32), (lane < 72).astype(jnp.int32))
            edge = jnp.where(odd == 1, (lane < W).astype(jnp.int32), (lane >= 128 - W).astype(jnp.int32))
            known = jnp.where(beside, o_in, c_in)
            value = jnp.where(inside * known == 1, a, jnp.where(edge * near_in * known == 1, b, 0.0))
            collect[o, pl.ds(q, 10, stride=4), :] = pltpu.roll(value, W + 64 * odd, 1)
            warm = sea[c, half, 10:14, :] * c_in.astype(f32)
            turn = pltpu.roll(warm, 64, 1)
            straight = jnp.where(odd == 1, turn, warm)
            crossed = jnp.where(odd == 1, warm, turn)
            for i in range(2):
                pair = jnp.where(lane2 < 64, straight[2 * i : 2 * i + 1], crossed[2 * i + 1 : 2 * i + 2])
                collect[o, 40 + 4 * i + q : 41 + 4 * i + q, :] = pair
        return 0

    lax.fori_loop(0, count, cut, 0, unroll=M)
    for o in range(count):
        out[o] = collect[o].astype(bf16)


def ice_kernel(got, nat, conc, vol, motion, stress, grown, out, wide, ext, temp, flux):
    for m in range(M):
        wide[m] = got[m].astype(f32)
    lane = lanes((8, 128))

    def rim(m, j):
        return wide[m, 4 * j : 4 * j + 4, :]

    def two(a, b):
        return jnp.concatenate([a, b], axis=0)

    def natural(f, r):
        return two(
            nat[f, :, 128 * r : 128 * r + 128], nat[f, :, 128 * (r + 16) : 128 * (r + 16) + 128]
        )

    for f in range(11):
        ext[f, 0] = jnp.zeros((8, 128), f32)
        ext[f, 49] = jnp.zeros((8, 128), f32)
    inside = (lane >= W) & (lane < W + BS)
    for r in range(16):
        t = r % 8
        for p in range(2):
            own = (lane >> 3) == 8 * p + t
            for f in range(NF):
                north = two(rim(8 + r // 8, 15 + f), rim(10 + r // 8, 15 + f))
                south = two(rim(12 + r // 8, 15 + f), rim(14 + r // 8, 15 + f))
                sides = roll(jnp.where(own, north, south), -(56 + 64 * p + 8 * t))
                ext[f, 9 + 2 * r + p] = jnp.where(inside, roll(natural(f, r), 8 - 64 * p), sides)
    for f in range(NF):
        for y in range(8):
            p, i = y % 2, f % 4
            centre = two(rim(4 + y // 2, 15 + f), rim(y // 2, 15 + f))
            corner = two(rim(4 + y // 2, 12 + f // 4), rim(y // 2, 12 + f // 4))
            value = jnp.where(
                inside, roll(centre, 8 - 64 * p), roll(corner, -(56 + 64 * p + 16 * i))
            )
            ext[f, 1 + y] = two(value[0:4], ext[f, 33 + y, 0:4, :])
            ext[f, 41 + y] = two(ext[f, 9 + y, 4:8, :], value[4:8])
    for y in range(48):
        for k in range(2):
            a, b = y, y + 32
            value = two(rim(a // 5, 5 * k + a % 5), rim(b // 5, 5 * k + b % 5))
            ext[9 + k, 1 + y] = value
            ext[2 + k, 1 + y] = ext[2 + k, 1 + y] + value
    thick = ext[0, 1:49]
    ext[11, 1:49] = jnp.where(thick > 0.0, 1.0 / (thick + 1.0), 0.0)
    ext[1, 1:49] = jnp.where(thick > 0.0, 0.5 * ext[1, 1:49], 0.0)

    step = 8

    def speed(i, _):
        at = pl.ds(1 + i * step, step)
        full = pl.ds(i * step, step + 2)
        one, two_, shear = ext[6, full], ext[7, full], ext[8, full]
        add = one + two_
        sub = one[1:-1] - two_[1:-1]
        mid = shear[1:-1]
        fx = 0.25 * (add[2:] - add[:-2]) + 0.5 * (roll(mid, -1) - roll(mid, 1))
        fy = 0.5 * (shear[2:] - shear[:-2]) + 0.25 * (roll(sub, -1) - roll(sub, 1))
        thick, inverse = ext[0, at], ext[11, at]
        u, v = ext[4, at], ext[5, at]
        half = 0.5 * thick
        ext[4, at] = (thick * u + fx + ext[2, at] + half * v) * inverse
        ext[5, at] = (thick * v + fy + ext[3, at] - half * u) * inverse
        return 0

    def strain(i, _):
        at = pl.ds(1 + i * step, step)
        full = pl.ds(i * step, step + 2)
        uu, vv = ext[4, full], ext[5, full]
        u, v = uu[1:-1], vv[1:-1]
        ux = uu[2:] - uu[:-2]
        vx = vv[2:] - vv[:-2]
        uy = roll(u, -1) - roll(u, 1)
        vy = roll(v, -1) - roll(v, 1)
        divergence = 0.5 * (ux + vy)
        tension = 0.5 * (ux - vy)
        shearing = 0.5 * (uy + vx)
        inverse = lax.rsqrt(
            divergence * divergence + 0.25 * (tension * tension + shearing * shearing) + 0.01
        )
        half = jnp.where(ext[0, at] > 0.0, 0.5, 0.0)
        strong = ext[1, at]
        scaled = strong * inverse
        ext[6, at] = half * ext[6, at] + (scaled * divergence - strong)
        ext[7, at] = half * ext[7, at] + 0.25 * scaled * tension
        ext[8, at] = half * ext[8, at] + 0.125 * scaled * shearing
        return 0

    for _ in range(SUBCYCLES):
        for i in range(48 // step):
            speed(i, 0)
        for i in range(48 // step):
            strain(i, 0)

    def flat(f, r):
        a, b = ext[f, 9 + 2 * r], ext[f, 10 + 2 * r]
        return jnp.where(lane < 64, roll(a, -8), roll(b, 56))

    for r in range(32):
        temp[:, 128 * r : 128 * r + 128] = rim(r // 2, 10 + r % 2)
    for r in range(16):
        for f in range(3):
            value = flat(6 + f, r)
            stress[f, :, 128 * r : 128 * r + 128] = value[0:4]
            stress[f, :, 128 * (r + 16) : 128 * (r + 16) + 128] = value[4:8]
        cover, ice = natural(9, r), natural(0, r) > 0.0
        for f in range(2):
            value = flat(4 + f, r)
            motion[:, f, 128 * r : 128 * r + 128] = value[0:4]
            motion[:, f, 128 * (r + 16) : 128 * (r + 16) + 128] = value[4:8]
            tau = jnp.where(ice, cover * (value - flat(9 + f, r)), 0.0)
            at = 4 * ((f + 1) * 2 + r % 2)
            flux[r // 2, at : at + 4, :] = tau[0:4]
            flux[8 + r // 2, at : at + 4, :] = tau[4:8]
    step = 512
    for start in range(0, BS * BS, step):
        sl = pl.ds(start, step)
        excess = temp[:, sl] + 1.8
        half = jnp.where(nat[0, :, sl] > 0.0, 0.5, 0.0)
        heat = jnp.zeros((4, step), f32)
        for n in range(conc.shape[0]):
            volume = vol[n, :, sl]
            rate = half * conc[n, :, sl] * ((1.5 - 0.5 * n) - excess) / (1.0 + volume)
            later = jnp.maximum(volume + rate, 0.0)
            grown[n, :, sl] = later
            heat = heat + (later - volume)
        for k in range(step // 128):
            r = start // 128 + k
            at = 4 * (r % 2)
            flux[r // 2, at : at + 4, :] = heat[:, 128 * k : 128 * k + 128]
    for m in range(M):
        out[m] = flux[m].astype(bf16)


def return_kernel(count, got, codes, out, pick, wide):
    for s in range(M):
        wide[ROWS3 * s : ROWS3 * s + ROWS3, :] = got[s].astype(f32)
    column = lax.broadcasted_iota(jnp.int32, (ROWS4, M * ROWS3), 0)
    local_code = (column & 7) * 8 + (column >> 3)
    span = codes[0:1, :]

    def build(c, _):
        base = pl.multiple_of(c * ROWS4, ROWS4)
        pick[pl.ds(base, ROWS4), :] = (span == local_code + c * 64).astype(bf16)
        return 0

    lax.fori_loop(0, count, build, 0)
    value = jnp.dot(pick[...], wide[...].astype(bf16), preferred_element_type=f32)
    out[...] = value.astype(bf16).reshape(count, ROWS4, 128)


def ocean_kernel(temp, drift, wet, before, after, temp_out, drift_out):
    levels = temp.shape[0]
    shape = temp.shape[1:]
    lane = lanes(shape)
    row = lax.broadcasted_iota(jnp.int32, shape, 0)
    sea = wet[...].astype(f32)
    for k in range(levels + drift.shape[0]):
        mid = temp[k] if k < levels else drift[k - levels]
        east = jnp.where(row == shape[0] - 1, after[k], roll(mid, -1, 0))
        west = jnp.where(row == 0, before[k], roll(mid, 1, 0))
        north = jnp.where(lane == shape[1] - 1, 0.0, roll(mid, -1))
        south = jnp.where(lane == 0, 0.0, roll(mid, 1))
        change = 0.2 * (east + west + north + south - 4.0 * mid)
        if k < levels:
            vertical = jnp.zeros(shape, f32)
            if k + 1 < levels:
                vertical = vertical + (temp[k + 1] - mid)
            if k > 0:
                vertical = vertical - (mid - temp[k - 1])
            temp_out[k] = mid + sea * (change + 0.2 * vertical)
        else:
            drift_out[k - levels] = mid + sea * change


def final_kernel(
    rows, got, wet, temp, drift, temp_out, drift_out, wide, flux, held, arrive, leave
):
    arrivals = []
    for k in range(3):
        place = temp.at[0] if k == 0 else drift.at[k - 1]
        arrivals.append(pltpu.make_async_copy(place, held.at[k], arrive.at[k]))
        arrivals[-1].start()
    for m in range(M):
        wide[pl.ds(ROWS4 * m, ROWS4), :] = got[m].astype(f32)
    flux[...] = jnp.zeros(flux.shape, f32)
    upper = lanes((M, 128)) >= 64
    for slot in range(KMAX):
        r = rows[slot]
        at = r // 2
        odd = lax.rem(r, 2) == 1
        keep = upper == odd
        for f in range(3):
            for h in range(2):
                value = wide[pl.ds(8 * (2 * f + h) + slot, M, stride=ROWS4), :]
                turned = roll(value, 64)
                for p in range(2):
                    chosen = jnp.where(odd, turned, value) if p == 0 else jnp.where(odd, value, turned)
                    to = (at, pl.ds(BS * f + 2 * h + p, M, stride=4), slice(None))
                    flux[to] = flux[to] + jnp.where(keep, chosen, 0.0)
    copies = []
    for k in range(3):
        arrivals[k].wait()
        for part in range(flux.shape[0]):
            cut = slice(128 * part, 128 * part + 128)
            added = wet[:, cut].astype(f32) * flux[part, BS * k : BS * (k + 1), :]
            held[k, :, cut] = held[k, :, cut] + added
        place = temp_out.at[0] if k == 0 else drift_out.at[k - 1]
        copies.append(pltpu.make_async_copy(held.at[k], place, leave.at[k]))
        copies[-1].start()
    for copy in copies:
        copy.wait()


def local(
    thermal_state,
    seawater_drift,
    sea_site_indicator,
    chosen_tile_numbers,
    chosen_floe_indicator,
    areal_fraction,
    thickness_amount,
    floe_motion,
    internal_traction,
    wind_traction,
):
    count = lax.axis_size("gx")
    groups = count // M
    me = lax.axis_index("gx")
    tiles = thermal_state.shape[2] // BS
    members = [[g * M + i for i in range(M)] for g in range(groups)]
    smem = pl.BlockSpec(memory_space=pltpu.SMEM)
    vmem = pl.BlockSpec(memory_space=pltpu.VMEM)
    depth, height = thermal_state.shape[1:]
    anywhere = pl.BlockSpec(memory_space=pl.ANY)
    top = pl.BlockSpec((1, depth, height), lambda i: (0, 0, 0))

    def whole(x):
        return pl.BlockSpec(x.shape, lambda i, n=len(x.shape): (0,) * n)

    def within(x):
        if groups == 1:
            return lax.all_to_all(x, "gx", 0, 0, tiled=True)
        return lax.all_to_all(x, "gx", 0, 0, axis_index_groups=members, tiled=True)

    def across(x):
        x = lax.all_to_all(x, "gx", 0, 0, tiled=True)
        if groups == 1:
            return x
        return jnp.sum(x.reshape((groups, M) + x.shape[1:]).astype(f32), 0).astype(bf16)

    tail = jnp.concatenate([thermal_state[:, depth - 1 :], seawater_drift[:, depth - 1 :]], 0)
    head = jnp.concatenate([thermal_state[:, :1], seawater_drift[:, :1]], 0)
    before = lax.ppermute(tail, "gx", [(i, (i + 1) % count) for i in range(count)])
    after = lax.ppermute(head, "gx", [((i + 1) % count, i) for i in range(count)])

    conc = jnp.transpose(areal_fraction, (1, 0, 2))
    vol = jnp.transpose(thickness_amount, (1, 0, 2))
    arrays = (
        thermal_state,
        seawater_drift,
        chosen_floe_indicator,
        conc,
        vol,
        floe_motion,
        jnp.transpose(internal_traction, (1, 0, 2)),
        wind_traction,
    )
    nat_shape = jax.ShapeDtypeStruct((10, 4, BS * BS), f32)
    one_shape = jax.ShapeDtypeStruct((M, ROWS1, 128), bf16)
    payload, nat = call(
        pack_kernel,
        (one_shape, nat_shape),
        scratch=(pltpu.VMEM((M, ROWS1, 128), f32),),
        grid=(1,),
        in_specs=[smem, top] + [whole(x) for x in arrays[1:]],
        out_specs=(whole(one_shape), whole(nat_shape)),
    )(chosen_tile_numbers, *arrays)
    got1 = within(payload)

    if groups == 1:
        everyone = got1
    else:
        mine = payload[0, 144:152]
        everyone = lax.all_gather(mine, "gx", axis=0, tiled=False)
    payload2 = call(
        functools.partial(route_kernel, count),
        pltpu.HBM((count, ROWS2, 128), bf16),
        scratch=(
            pltpu.VMEM((M, ROWS1, 128), f32),
            pltpu.VMEM((M, 8, 16, 128), f32),
            pltpu.VMEM((count, 128), jnp.int32),
            pltpu.SMEM((count, 128), jnp.int32),
            pltpu.VMEM((count, ROWS2, 128), f32),
            pltpu.SemaphoreType.DMA,
        ),
        in_specs=[smem, vmem, vmem],
        out_specs=vmem,
        vmem=ROOM,
    )(me.reshape(1).astype(jnp.int32), got1, everyone)
    got2 = across(payload2)

    pairs = everyone[:, everyone.shape[1] - 4, 0:8].astype(jnp.int32)
    columns, rows = pairs[:, :4].reshape(-1), pairs[:, 4:].reshape(-1)
    ranks = jnp.sum(
        ((columns[None, :] == columns[:, None]) & (rows[None, :] < rows[:, None])).astype(jnp.int32), 1
    )
    slot = jnp.arange(KMAX, dtype=jnp.int32)
    mine = (columns[None, :] == me) & (ranks[None, :] == slot[:, None])
    slot_rows = jnp.sum(jnp.where(mine, rows[None, :], 0), 1)
    code = columns * 64 + ranks * 8
    code = lax.dynamic_slice_in_dim(code, (me // M) * (M * 4), M * 4, 0)
    item = jnp.arange(6, dtype=jnp.int32)
    codes = (code.reshape(M, 1, 4) + item[None, :, None]).reshape(1, M * ROWS3)

    temp_new, drift_new = call(
        ocean_kernel,
        (
            jax.ShapeDtypeStruct(thermal_state.shape, f32),
            jax.ShapeDtypeStruct(seawater_drift.shape, f32),
        ),
        in_specs=[vmem] * 5,
        out_specs=(vmem, vmem),
        cost_estimate=pl.CostEstimate(flops=10**7, bytes_accessed=6 * 10**6, transcendentals=0),
    )(thermal_state, seawater_drift, sea_site_indicator, before, after)

    motion, stress, grown, payload3 = call(
        ice_kernel,
        (
            jax.ShapeDtypeStruct(floe_motion.shape, f32),
            jax.ShapeDtypeStruct(arrays[6].shape, f32),
            jax.ShapeDtypeStruct(vol.shape, f32),
            pltpu.HBM((M, ROWS3, 128), bf16),
        ),
        scratch=(
            pltpu.VMEM((M, ROWS2, 128), f32),
            pltpu.VMEM((12, 50, 8, 128), f32),
            pltpu.VMEM((4, BS * BS), f32),
            pltpu.VMEM((M, ROWS3, 128), f32),
        ),
        in_specs=[vmem] * 4,
        out_specs=(vmem,) * 4,
        vmem=ROOM,
    )(got2, nat, conc, vol)
    stress = jnp.transpose(stress, (1, 0, 2))
    grown = jnp.transpose(grown, (1, 0, 2))
    got3 = within(payload3)

    payload4 = call(
        functools.partial(return_kernel, count),
        pltpu.HBM((count, ROWS4, 128), bf16),
        scratch=(
            pltpu.VMEM((count * ROWS4, M * ROWS3), bf16),
            pltpu.VMEM((M * ROWS3, 128), f32),
        ),
        in_specs=[vmem, vmem],
        out_specs=vmem,
        vmem=ROOM,
    )(got3, codes)
    got4 = across(payload4)

    temp_later, drift_later = call(
        final_kernel,
        (
            jax.ShapeDtypeStruct(thermal_state.shape, f32),
            jax.ShapeDtypeStruct(seawater_drift.shape, f32),
        ),
        scratch=(
            pltpu.VMEM((M * ROWS4, 128), f32),
            pltpu.VMEM((height // 128, 3 * BS, 128), f32),
            pltpu.VMEM((3, depth, height), f32),
            pltpu.SemaphoreType.DMA((3,)),
            pltpu.SemaphoreType.DMA((3,)),
        ),
        in_specs=[smem, vmem, vmem, anywhere, anywhere],
        out_specs=(anywhere, anywhere),
        input_output_aliases={3: 0, 4: 1},
        vmem=ROOM,
    )(slot_rows, got4, sea_site_indicator, temp_new, drift_new)
    return temp_later, drift_later, motion, stress, grown


def solution(mesh):
    return jax.shard_map(
        local,
        mesh=mesh,
        in_specs=(
            P("member", "gx", None),
            P("member", "gx", None),
            P("gx", None),
            P(("member", "gx")),
            P(("member", "gx"), None),
            P(("member", "gx"), None, None),
            P(("member", "gx"), None, None),
            P(("member", "gx"), None, None),
            P(("member", "gx"), None, None),
            P(("member", "gx"), None, None),
        ),
        out_specs=(
            P("member", "gx", None),
            P("member", "gx", None),
            P(("member", "gx"), None, None),
            P(("member", "gx"), None, None),
            P(("member", "gx"), None, None),
        ),
        check_vma=False,
    )
```

```python
import functools

import jax
import jax.numpy as jnp
from jax import lax
from jax.experimental import pallas as pl
from jax.experimental.pallas import tpu as pltpu
from jax.sharding import PartitionSpec as P

BS = 64
SUBCYCLES = 4
KMAX = 8
M = 16
W = 8
NF = 9
ROWS1 = 136
ROWS2 = 88
ROWS3 = 24
ROWS4 = 48
SEA = 12
VMEM = 60 * 2**20
ROOM = 40 * 2**20
f32, bf16 = jnp.float32, jnp.bfloat16


def lanes(shape):
    return lax.broadcasted_iota(jnp.int32, shape, len(shape) - 1)


def roll(x, shift, axis=-1):
    axis = axis % x.ndim
    shift = shift % x.shape[axis]
    return x if shift == 0 else pltpu.roll(x, shift, axis)


def call(kernel, out_shape, scratch=(), in_specs=None, out_specs=None, vmem=VMEM, **kw):
    return pl.pallas_call(
        kernel,
        out_shape=out_shape,
        in_specs=in_specs,
        out_specs=out_specs,
        scratch_shapes=list(scratch),
        compiler_params=pltpu.CompilerParams(vmem_limit_bytes=vmem),
        **kw,
    )


def sea_rows(m):
    if m >= 8:
        return [(24 + 4 * (m - 8), 4)]
    return [(2 * m if m < 4 else 48 + 2 * m, 2), (8 + 2 * m, 2)]


def pack_kernel(ids, temp, drift, cells, conc, vol, motion, stress, wind, out, nat, big):
    tiles = temp.shape[2] // BS
    step = 512
    for start in range(0, BS * BS, step):
        sl = pl.ds(start, step)
        ice = cells[:, sl].astype(f32)
        cover = jnp.sum(conc[:, :, sl], axis=0)
        thick = jnp.sum(vol[:, :, sl], axis=0)
        nat[0, :, sl] = thick * ice
        nat[1, :, sl] = 2.0 * thick * jnp.exp(-5.0 * (1.0 - cover))
        nat[9, :, sl] = cover
        for k in range(2):
            nat[2 + k, :, sl] = wind[:, k, sl]
            nat[4 + k, :, sl] = motion[:, k, sl]
        for k in range(3):
            nat[6 + k, :, sl] = stress[k, :, sl]
    lane = lanes((4, 128))
    low, high = (lane & 63) < W, (lane & 63) >= BS - W
    lane_all = lanes((4, 128))
    row_all = lax.broadcasted_iota(jnp.int32, (4, 128), 0)
    listed = jnp.zeros((4, 128), f32)
    for q in range(4):
        number = ids[q]
        column, row = number // tiles, number % tiles
        listed = jnp.where(lane_all == q, column.astype(f32), listed)
        listed = jnp.where(lane_all == 4 + q, row.astype(f32), listed)
    listed = jnp.where(row_all == 0, listed, 0.0)
    for m in range(M):
        big[m, 132:136, :] = listed
        for part in range(8):
            cut = slice(128 * part, 128 * part + 128)
            at = SEA * part
            for k in range(2):
                place = at + 4 * k
                for start, size in sea_rows(m):
                    big[m, place : place + size, :] = drift[k, start : start + size, cut]
                    place += size
            big[m, at + 8 : at + 12, :] = temp[0, 4 * m : 4 * m + 4, cut]
    for f in range(NF):
        at = slice(96 + 4 * f, 100 + 4 * f)
        for k in range(4):
            big[k, at, :] = nat[f, :, 128 * k : 128 * k + 128]
            big[4 + k, at, :] = nat[f, :, 3584 + 128 * k : 3712 + 128 * k]
            first = jnp.zeros((4, 128), f32)
            last = jnp.zeros((4, 128), f32)
            for t in range(8):
                v = nat[f, :, 128 * (8 * k + t) : 128 * (8 * k + t) + 128]
                first = first + roll(jnp.where(low, v, 0.0), 8 * t)
                last = last + roll(jnp.where(high, v, 0.0), 8 * t)
            big[8 + k, at, :] = first
            big[12 + k, at, :] = last
    for m in range(M):
        out[m] = big[m].astype(bf16)


def route_kernel(count, me, got, everyone, out, wide, sea, listed, numbers, collect, field, sem):
    for s in range(M):
        wide[s] = got[s].astype(f32)
    if count == M:
        listed[...] = wide[:, 132, :].astype(jnp.int32)
    else:
        listed[...] = everyone[...].astype(f32)[:, 4, :].astype(jnp.int32)
    copy = pltpu.make_async_copy(listed, numbers, sem)
    copy.start()
    me_now = me[0]
    m = lax.rem(me_now, M)
    first = me_now - m
    for s in range(M):
        for part in range(8):
            sea[s, part, 0:SEA, :] = wide[s, SEA * part : SEA * part + SEA, :]

    east = m < 4
    west = jnp.logical_and(m >= 4, m < 8)
    north = jnp.logical_and(m >= 8, m < 12)
    shift_c = jnp.where(east, 1, jnp.where(west, -1, 0))
    shift_r = jnp.where(north, 1, jnp.where(m >= 12, -1, 0))
    size = count * 4
    spread = jnp.broadcast_to(listed[...].astype(f32)[:, None, :], (count, 4, 128))
    spread = spread.reshape(size, 128)
    q_of = lax.broadcasted_iota(jnp.int32, (size, 128), 0) & 3
    lane_of = lanes((size, 128))
    column = jnp.sum(jnp.where(lane_of == q_of, spread, 0.0), axis=1, keepdims=True)
    row = jnp.sum(jnp.where(lane_of == q_of + 4, spread, 0.0), axis=1, keepdims=True)
    eye = lax.broadcasted_iota(jnp.int32, (size, size), 0) == lanes((size, size))
    number = jnp.sum(jnp.where(eye, column * 16.0 + row, 0.0), axis=0, keepdims=True)
    tc = column + shift_c.astype(f32)
    tc = jnp.where(tc < 0, tc + count, tc)
    tc = jnp.where(tc >= count, tc - count, tc)
    tr = row + shift_r.astype(f32)

    def one_hot(r):
        code = jnp.where((r >= 0) & (r < 16), tc * 16.0 + r, -1.0)
        return (code == number).astype(bf16)

    centre = one_hot(tr)
    before = one_hot(jnp.where(tr >= 0, tr - 1.0, -1.0))
    after = one_hot(jnp.where(tr < 16, tr + 1.0, 16.0))

    copy.wait()
    lane = lanes((8, 128))
    lane2 = lanes((1, 128))

    def cut(o, _):
        for q in range(4):
            c, r = numbers[o, q] - first, numbers[o, 4 + q]
            known = jnp.logical_and(c >= 0, c < M).astype(jnp.int32)
            c = jnp.clip(c, 0, M - 1)
            half, odd = r >> 1, r & 1
            near = half + 2 * odd - 1
            near_in = jnp.logical_and(near >= 0, near < 8).astype(jnp.int32)
            near = jnp.clip(near, 0, 7)
            a, b = sea[c, half, 0:8, :], sea[c, near, 0:8, :]
            inside = jnp.where(odd == 1, (lane >= 56).astype(jnp.int32), (lane < 72).astype(jnp.int32))
            edge = jnp.where(odd == 1, (lane < W).astype(jnp.int32), (lane >= 128 - W).astype(jnp.int32))
            value = jnp.where(inside * known == 1, a, jnp.where(edge * near_in * known == 1, b, 0.0))
            collect[o, pl.ds(q, 8, stride=4), :] = pltpu.roll(value, W + 64 * odd, 1)
            warm = sea[c, half, 8:12, :] * known.astype(f32)
            turn = pltpu.roll(warm, 64, 1)
            straight = jnp.where(odd == 1, turn, warm)
            crossed = jnp.where(odd == 1, warm, turn)
            for i in range(2):
                pair = jnp.where(lane2 < 64, straight[2 * i : 2 * i + 1], crossed[2 * i + 1 : 2 * i + 2])
                collect[o, 32 + 4 * i + q : 33 + 4 * i + q, :] = pair
        return 0

    lax.fori_loop(0, count, cut, 0, unroll=M)

    lane = lanes((size, 128))
    low, high = (lane & 63) < W, (lane & 63) >= BS - W
    rim = (m < 8).astype(f32)
    for jj in range(3):
        first_part = jnp.zeros((size, 128), f32)
        last_part = jnp.zeros((size, 128), f32)
        for i in range(min(4, NF - 4 * jj)):
            f = 4 * jj + i
            own = wide[:, 96 + 4 * f : 100 + 4 * f, :]
            if count > M:
                field[...] = jnp.zeros(field.shape, f32)
                field[pl.ds(first, M)] = own
                own = field[...]
            own = own.reshape(size, 128)
            if f in (2, 3):
                at = 16 * (f - 2)
                one = roll(collect[:, at : at + 4, :], -W).reshape(size, 128)
                two = roll(collect[:, at + 4 : at + 8, :], 64 - W).reshape(size, 128)
                own = own + rim * jnp.where(lane < 64, one, two)
            value = jnp.dot(centre, own.astype(bf16), preferred_element_type=f32)
            collect[:, 52 + 4 * f : 56 + 4 * f, :] = value.reshape(count, 4, 128)
            last_part = last_part + roll(jnp.where(high, own, 0.0), 16 * i)
            first_part = first_part + roll(jnp.where(low, own, 0.0), 16 * i)
        value = jnp.dot(before, last_part.astype(bf16), preferred_element_type=f32)
        value = value + jnp.dot(after, first_part.astype(bf16), preferred_element_type=f32)
        collect[:, 40 + 4 * jj : 44 + 4 * jj, :] = value.reshape(count, 4, 128)
    for o in range(count):
        out[o] = collect[o].astype(bf16)


def ice_kernel(got, nat, conc, vol, motion, stress, grown, out, wide, ext, temp, flux):
    for m in range(M):
        wide[m] = got[m].astype(f32)
    lane = lanes((8, 128))

    def rim(m, j):
        return wide[m, 4 * j : 4 * j + 4, :]

    def two(a, b):
        return jnp.concatenate([a, b], axis=0)

    def natural(f, r):
        return two(
            nat[f, :, 128 * r : 128 * r + 128], nat[f, :, 128 * (r + 16) : 128 * (r + 16) + 128]
        )

    for f in range(11):
        ext[f, 0] = jnp.zeros((8, 128), f32)
        ext[f, 49] = jnp.zeros((8, 128), f32)
    inside = (lane >= W) & (lane < W + BS)
    for r in range(16):
        t = r % 8
        for p in range(2):
            own = (lane >> 3) == 8 * p + t
            for f in range(NF):
                north = two(rim(8 + r // 8, 13 + f), rim(10 + r // 8, 13 + f))
                south = two(rim(12 + r // 8, 13 + f), rim(14 + r // 8, 13 + f))
                sides = roll(jnp.where(own, north, south), -(56 + 64 * p + 8 * t))
                ext[f, 9 + 2 * r + p] = jnp.where(inside, roll(natural(f, r), 8 - 64 * p), sides)
    for f in range(NF):
        for y in range(8):
            p, i = y % 2, f % 4
            centre = two(rim(4 + y // 2, 13 + f), rim(y // 2, 13 + f))
            corner = two(rim(4 + y // 2, 10 + f // 4), rim(y // 2, 10 + f // 4))
            value = jnp.where(
                inside, roll(centre, 8 - 64 * p), roll(corner, -(56 + 64 * p + 16 * i))
            )
            ext[f, 1 + y] = two(value[0:4], ext[f, 33 + y, 0:4, :])
            ext[f, 41 + y] = two(ext[f, 9 + y, 4:8, :], value[4:8])
    where = {}
    for m in range(M):
        listed = [start + i for start, size in sea_rows(m) for i in range(size)]
        for k, row in enumerate(listed):
            where[row + W] = (m, k)
    blank = jnp.zeros((4, 128), f32)
    for y in range(48):
        for k in range(2):
            halves = [where.get(x) for x in (y, y + 32)]
            halves = [blank if at is None else rim(at[0], 4 * k + at[1]) for at in halves]
            value = two(*halves)
            ext[9 + k, 1 + y] = value
            ext[2 + k, 1 + y] = ext[2 + k, 1 + y] + value
    thick = ext[0, 1:49]
    ext[11, 1:49] = jnp.where(thick > 0.0, 1.0 / (thick + 1.0), 0.0)
    ext[1, 1:49] = jnp.where(thick > 0.0, 0.5 * ext[1, 1:49], 0.0)

    step = 8

    def speed(i, _):
        at = pl.ds(1 + i * step, step)
        full = pl.ds(i * step, step + 2)
        one, two_, shear = ext[6, full], ext[7, full], ext[8, full]
        add = one + two_
        sub = one[1:-1] - two_[1:-1]
        mid = shear[1:-1]
        fx = 0.25 * (add[2:] - add[:-2]) + 0.5 * (roll(mid, -1) - roll(mid, 1))
        fy = 0.5 * (shear[2:] - shear[:-2]) + 0.25 * (roll(sub, -1) - roll(sub, 1))
        thick, inverse = ext[0, at], ext[11, at]
        u, v = ext[4, at], ext[5, at]
        half = 0.5 * thick
        ext[4, at] = (thick * u + fx + ext[2, at] + half * v) * inverse
        ext[5, at] = (thick * v + fy + ext[3, at] - half * u) * inverse
        return 0

    def strain(i, _):
        at = pl.ds(1 + i * step, step)
        full = pl.ds(i * step, step + 2)
        uu, vv = ext[4, full], ext[5, full]
        u, v = uu[1:-1], vv[1:-1]
        ux = uu[2:] - uu[:-2]
        vx = vv[2:] - vv[:-2]
        uy = roll(u, -1) - roll(u, 1)
        vy = roll(v, -1) - roll(v, 1)
        divergence = 0.5 * (ux + vy)
        tension = 0.5 * (ux - vy)
        shearing = 0.5 * (uy + vx)
        inverse = lax.rsqrt(
            divergence * divergence + 0.25 * (tension * tension + shearing * shearing) + 0.01
        )
        half = jnp.where(ext[0, at] > 0.0, 0.5, 0.0)
        strong = ext[1, at]
        scaled = strong * inverse
        ext[6, at] = half * ext[6, at] + (scaled * divergence - strong)
        ext[7, at] = half * ext[7, at] + 0.25 * scaled * tension
        ext[8, at] = half * ext[8, at] + 0.125 * scaled * shearing
        return 0

    for _ in range(SUBCYCLES):
        for i in range(48 // step):
            speed(i, 0)
        for i in range(48 // step):
            strain(i, 0)

    def flat(f, r):
        a, b = ext[f, 9 + 2 * r], ext[f, 10 + 2 * r]
        return jnp.where(lane < 64, roll(a, -8), roll(b, 56))

    for r in range(32):
        temp[:, 128 * r : 128 * r + 128] = rim(r // 2, 8 + r % 2)
    for r in range(16):
        for f in range(3):
            value = flat(6 + f, r)
            stress[f, :, 128 * r : 128 * r + 128] = value[0:4]
            stress[f, :, 128 * (r + 16) : 128 * (r + 16) + 128] = value[4:8]
        cover, ice = natural(9, r), natural(0, r) > 0.0
        for f in range(2):
            value = flat(4 + f, r)
            motion[:, f, 128 * r : 128 * r + 128] = value[0:4]
            motion[:, f, 128 * (r + 16) : 128 * (r + 16) + 128] = value[4:8]
            tau = jnp.where(ice, cover * (value - flat(9 + f, r)), 0.0)
            at = 4 * ((f + 1) * 2 + r % 2)
            flux[r // 2, at : at + 4, :] = tau[0:4]
            flux[8 + r // 2, at : at + 4, :] = tau[4:8]
    step = 512
    for start in range(0, BS * BS, step):
        sl = pl.ds(start, step)
        excess = temp[:, sl] + 1.8
        half = jnp.where(nat[0, :, sl] > 0.0, 0.5, 0.0)
        heat = jnp.zeros((4, step), f32)
        for n in range(conc.shape[0]):
            volume = vol[n, :, sl]
            rate = half * conc[n, :, sl] * ((1.5 - 0.5 * n) - excess) / (1.0 + volume)
            later = jnp.maximum(volume + rate, 0.0)
            grown[n, :, sl] = later
            heat = heat + (later - volume)
        for k in range(step // 128):
            r = start // 128 + k
            at = 4 * (r % 2)
            flux[r // 2, at : at + 4, :] = heat[:, 128 * k : 128 * k + 128]
    for m in range(M):
        out[m] = flux[m].astype(bf16)


def return_kernel(count, got, codes, out, pick, wide):
    for s in range(M):
        wide[ROWS3 * s : ROWS3 * s + ROWS3, :] = got[s].astype(f32)
    column = lax.broadcasted_iota(jnp.int32, (ROWS4, M * ROWS3), 0)
    local_code = (column & 7) * 8 + (column >> 3)
    span = codes[0:1, :]

    def build(c, _):
        base = pl.multiple_of(c * ROWS4, ROWS4)
        pick[pl.ds(base, ROWS4), :] = (span == local_code + c * 64).astype(bf16)
        return 0

    lax.fori_loop(0, count, build, 0)
    value = jnp.dot(pick[...], wide[...].astype(bf16), preferred_element_type=f32)
    out[...] = value.astype(bf16).reshape(count, ROWS4, 128)


def ocean_kernel(temp, drift, wet, before, after, _, temp_out, drift_out):
    levels = temp.shape[0]
    shape = temp.shape[1:]
    lane = lanes(shape)
    row = lax.broadcasted_iota(jnp.int32, shape, 0)
    sea = wet[...].astype(f32)
    for k in range(levels + drift.shape[0]):
        mid = temp[k] if k < levels else drift[k - levels]
        east = jnp.where(row == shape[0] - 1, after[k], roll(mid, -1, 0))
        west = jnp.where(row == 0, before[k], roll(mid, 1, 0))
        north = jnp.where(lane == shape[1] - 1, 0.0, roll(mid, -1))
        south = jnp.where(lane == 0, 0.0, roll(mid, 1))
        change = 0.2 * (east + west + north + south - 4.0 * mid)
        if k < levels:
            vertical = jnp.zeros(shape, f32)
            if k + 1 < levels:
                vertical = vertical + (temp[k + 1] - mid)
            if k > 0:
                vertical = vertical - (mid - temp[k - 1])
            temp_out[k] = mid + sea * (change + 0.2 * vertical)
        else:
            drift_out[k - levels] = mid + sea * change


def final_kernel(
    rows, got, wet, temp, drift, temp_out, drift_out, wide, flux, held, arrive, leave
):
    arrivals = []
    for k in range(3):
        place = temp.at[0] if k == 0 else drift.at[k - 1]
        arrivals.append(pltpu.make_async_copy(place, held.at[k], arrive.at[k]))
        arrivals[-1].start()
    for m in range(M):
        wide[pl.ds(ROWS4 * m, ROWS4), :] = got[m].astype(f32)
    flux[0:16] = jnp.zeros((16,) + flux.shape[1:], f32)
    for slot in range(KMAX):
        r = rows[slot]
        for f in range(3):
            for h in range(2):
                value = wide[pl.ds(8 * (2 * f + h) + slot, M, stride=ROWS4), :]
                flux[r, pl.ds(BS * f + 2 * h, M, stride=4), :] = value
                flux[r, pl.ds(BS * f + 2 * h + 1, M, stride=4), :] = roll(value, 64)
    left = lanes((BS, 128)) < 64
    copies = []
    for k in range(3):
        arrivals[k].wait()
        for part in range(8):
            cut = slice(128 * part, 128 * part + 128)
            rows_of = slice(BS * k, BS * (k + 1))
            pair = jnp.where(left, flux[2 * part, rows_of, :], roll(flux[2 * part + 1, rows_of, :], 64))
            added = wet[:, cut].astype(f32) * pair
            held[k, :, cut] = held[k, :, cut] + added
        place = temp_out.at[0] if k == 0 else drift_out.at[k - 1]
        copies.append(pltpu.make_async_copy(held.at[k], place, leave.at[k]))
        copies[-1].start()
    for copy in copies:
        copy.wait()


def local(
    thermal_state,
    seawater_drift,
    sea_site_indicator,
    chosen_tile_numbers,
    chosen_floe_indicator,
    areal_fraction,
    thickness_amount,
    floe_motion,
    internal_traction,
    wind_traction,
):
    count = lax.axis_size("gx")
    groups = count // M
    me = lax.axis_index("gx")
    tiles = thermal_state.shape[2] // BS
    members = [[g * M + i for i in range(M)] for g in range(groups)]
    smem = pl.BlockSpec(memory_space=pltpu.SMEM)
    vmem = pl.BlockSpec(memory_space=pltpu.VMEM)
    depth, height = thermal_state.shape[1:]
    anywhere = pl.BlockSpec(memory_space=pl.ANY)
    top = pl.BlockSpec((1, depth, height), lambda i: (0, 0, 0))

    def whole(x):
        return pl.BlockSpec(x.shape, lambda i, n=len(x.shape): (0,) * n)

    def within(x):
        if groups == 1:
            return lax.all_to_all(x, "gx", 0, 0, tiled=True)
        return lax.all_to_all(x, "gx", 0, 0, axis_index_groups=members, tiled=True)

    def across(x):
        x = lax.all_to_all(x, "gx", 0, 0, tiled=True)
        if groups == 1:
            return x
        return jnp.sum(x.reshape((groups, M) + x.shape[1:]).astype(f32), 0).astype(bf16)

    tail = jnp.concatenate([thermal_state[:, depth - 1 :], seawater_drift[:, depth - 1 :]], 0)
    head = jnp.concatenate([thermal_state[:, :1], seawater_drift[:, :1]], 0)
    before = lax.ppermute(tail, "gx", [(i, (i + 1) % count) for i in range(count)])
    after = lax.ppermute(head, "gx", [((i + 1) % count, i) for i in range(count)])

    conc = jnp.transpose(areal_fraction, (1, 0, 2))
    vol = jnp.transpose(thickness_amount, (1, 0, 2))
    arrays = (
        thermal_state,
        seawater_drift,
        chosen_floe_indicator,
        conc,
        vol,
        floe_motion,
        jnp.transpose(internal_traction, (1, 0, 2)),
        wind_traction,
    )
    nat_shape = jax.ShapeDtypeStruct((10, 4, BS * BS), f32)
    one_shape = jax.ShapeDtypeStruct((M, ROWS1, 128), bf16)
    payload, nat = call(
        pack_kernel,
        (one_shape, nat_shape),
        scratch=(pltpu.VMEM((M, ROWS1, 128), f32),),
        grid=(1,),
        in_specs=[smem, top] + [whole(x) for x in arrays[1:]],
        out_specs=(whole(one_shape), whole(nat_shape)),
    )(chosen_tile_numbers, *arrays)
    got1 = within(payload)

    if groups == 1:
        everyone = got1
    else:
        mine = payload[0, 128:136]
        everyone = lax.all_gather(mine, "gx", axis=0, tiled=False)
    payload2 = call(
        functools.partial(route_kernel, count),
        pltpu.HBM((count, ROWS2, 128), bf16),
        scratch=(
            pltpu.VMEM((M, ROWS1, 128), f32),
            pltpu.VMEM((M, 8, 16, 128), f32),
            pltpu.VMEM((count, 128), jnp.int32),
            pltpu.SMEM((count, 128), jnp.int32),
            pltpu.VMEM((count, ROWS2, 128), f32),
            pltpu.VMEM((count, 4, 128), f32),
            pltpu.SemaphoreType.DMA,
        ),
        in_specs=[smem, vmem, vmem],
        out_specs=vmem,
        vmem=ROOM,
    )(me.reshape(1).astype(jnp.int32), got1, everyone)
    got2 = across(payload2)

    pairs = everyone[:, everyone.shape[1] - 4, 0:8].astype(jnp.int32)
    columns, rows = pairs[:, :4].reshape(-1), pairs[:, 4:].reshape(-1)
    ranks = jnp.sum(
        ((columns[None, :] == columns[:, None]) & (rows[None, :] < rows[:, None])).astype(jnp.int32), 1
    )
    slot = jnp.arange(KMAX, dtype=jnp.int32)
    mine = (columns[None, :] == me) & (ranks[None, :] == slot[:, None])
    slot_rows = 16 + jnp.sum(jnp.where(mine, rows[None, :] - 16, 0), 1)
    code = columns * 64 + ranks * 8
    code = lax.dynamic_slice_in_dim(code, (me // M) * (M * 4), M * 4, 0)
    item = jnp.arange(6, dtype=jnp.int32)
    codes = (code.reshape(M, 1, 4) + item[None, :, None]).reshape(1, M * ROWS3)

    motion, stress, grown, payload3 = call(
        ice_kernel,
        (
            jax.ShapeDtypeStruct(floe_motion.shape, f32),
            jax.ShapeDtypeStruct(arrays[6].shape, f32),
            jax.ShapeDtypeStruct(vol.shape, f32),
            pltpu.HBM((M, ROWS3, 128), bf16),
        ),
        scratch=(
            pltpu.VMEM((M, ROWS2, 128), f32),
            pltpu.VMEM((12, 50, 8, 128), f32),
            pltpu.VMEM((4, BS * BS), f32),
            pltpu.VMEM((M, ROWS3, 128), f32),
        ),
        in_specs=[vmem] * 4,
        out_specs=(vmem,) * 4,
        vmem=ROOM,
    )(got2, nat, conc, vol)
    stress = jnp.transpose(stress, (1, 0, 2))
    grown = jnp.transpose(grown, (1, 0, 2))
    temp_new, drift_new = call(
        ocean_kernel,
        (
            jax.ShapeDtypeStruct(thermal_state.shape, f32),
            jax.ShapeDtypeStruct(seawater_drift.shape, f32),
        ),
        in_specs=[vmem] * 5 + [anywhere],
        out_specs=(vmem, vmem),
        cost_estimate=pl.CostEstimate(flops=10**7, bytes_accessed=6 * 10**6, transcendentals=0),
    )(thermal_state, seawater_drift, sea_site_indicator, before, after, payload3)

    got3 = within(payload3)

    payload4 = call(
        functools.partial(return_kernel, count),
        pltpu.HBM((count, ROWS4, 128), bf16),
        scratch=(
            pltpu.VMEM((count * ROWS4, M * ROWS3), bf16),
            pltpu.VMEM((M * ROWS3, 128), f32),
        ),
        in_specs=[vmem, vmem],
        out_specs=vmem,
        vmem=ROOM,
    )(got3, codes)
    got4 = across(payload4)

    temp_later, drift_later = call(
        final_kernel,
        (
            jax.ShapeDtypeStruct(thermal_state.shape, f32),
            jax.ShapeDtypeStruct(seawater_drift.shape, f32),
        ),
        scratch=(
            pltpu.VMEM((M * ROWS4, 128), f32),
            pltpu.VMEM((17, 3 * BS, 128), f32),
            pltpu.VMEM((3, depth, height), f32),
            pltpu.SemaphoreType.DMA((3,)),
            pltpu.SemaphoreType.DMA((3,)),
        ),
        in_specs=[smem, vmem, vmem, anywhere, anywhere],
        out_specs=(anywhere, anywhere),
        input_output_aliases={3: 0, 4: 1},
        vmem=ROOM,
    )(slot_rows, got4, sea_site_indicator, temp_new, drift_new)
    return temp_later, drift_later, motion, stress, grown


def solution(mesh):
    return jax.shard_map(
        local,
        mesh=mesh,
        in_specs=(
            P("member", "gx", None),
            P("member", "gx", None),
            P("gx", None),
            P(("member", "gx")),
            P(("member", "gx"), None),
            P(("member", "gx"), None, None),
            P(("member", "gx"), None, None),
            P(("member", "gx"), None, None),
            P(("member", "gx"), None, None),
            P(("member", "gx"), None, None),
        ),
        out_specs=(
            P("member", "gx", None),
            P("member", "gx", None),
            P(("member", "gx"), None, None),
            P(("member", "gx"), None, None),
            P(("member", "gx"), None, None),
        ),
        check_vma=False,
    )
```

```python
import functools

import jax
import jax.numpy as jnp
from jax import lax
from jax.experimental import pallas as pl
from jax.experimental.pallas import tpu as pltpu
from jax.sharding import PartitionSpec as P

BS = 64
SUBCYCLES = 4
KMAX = 8
M = 16
W = 8
NF = 9
ROWS1 = 136
ROWS2 = 80
ROWS3 = 24
ROWS4 = 48
FREE = BS + 2 * W
SEA = 12
VMEM = 60 * 2**20
ROOM = 40 * 2**20
f32, bf16 = jnp.float32, jnp.bfloat16


def lanes(shape):
    return lax.broadcasted_iota(jnp.int32, shape, len(shape) - 1)


def roll(x, shift, axis=-1):
    axis = axis % x.ndim
    shift = shift % x.shape[axis]
    return x if shift == 0 else pltpu.roll(x, shift, axis)


def call(kernel, out_shape, scratch=(), in_specs=None, out_specs=None, vmem=VMEM, **kw):
    return pl.pallas_call(
        kernel,
        out_shape=out_shape,
        in_specs=in_specs,
        out_specs=out_specs,
        scratch_shapes=list(scratch),
        compiler_params=pltpu.CompilerParams(vmem_limit_bytes=vmem),
        **kw,
    )


def sea_rows(m):
    if m >= 8:
        return [(24 + 4 * (m - 8), 4)]
    return [(2 * m if m < 4 else 48 + 2 * m, 2), (8 + 2 * m, 2)]


def pack_kernel(ids, temp, drift, cells, conc, vol, motion, stress, wind, out, nat, big):
    tiles = temp.shape[2] // BS
    step = 512
    for start in range(0, BS * BS, step):
        sl = pl.ds(start, step)
        ice = cells[:, sl].astype(f32)
        cover = jnp.sum(conc[:, :, sl], axis=0)
        thick = jnp.sum(vol[:, :, sl], axis=0)
        nat[0, :, sl] = thick * ice
        nat[1, :, sl] = 2.0 * thick * jnp.exp(-5.0 * (1.0 - cover))
        nat[9, :, sl] = cover
        for k in range(2):
            nat[2 + k, :, sl] = wind[:, k, sl]
            nat[4 + k, :, sl] = motion[:, k, sl]
        for k in range(3):
            nat[6 + k, :, sl] = stress[k, :, sl]
    lane = lanes((4, 128))
    low, high = (lane & 63) < W, (lane & 63) >= BS - W
    lane_all = lanes((4, 128))
    row_all = lax.broadcasted_iota(jnp.int32, (4, 128), 0)
    listed = jnp.zeros((4, 128), f32)
    for q in range(4):
        number = ids[q]
        column, row = number // tiles, number % tiles
        listed = jnp.where(lane_all == q, column.astype(f32), listed)
        listed = jnp.where(lane_all == 4 + q, row.astype(f32), listed)
    listed = jnp.where(row_all == 0, listed, 0.0)
    for m in range(M):
        big[m, 132:136, :] = listed
        for part in range(8):
            cut = slice(128 * part, 128 * part + 128)
            at = SEA * part
            for k in range(2):
                place = at + 4 * k
                for start, size in sea_rows(m):
                    big[m, place : place + size, :] = drift[k, start : start + size, cut]
                    place += size
            big[m, at + 8 : at + 12, :] = temp[0, 4 * m : 4 * m + 4, cut]
    for f in range(NF):
        at = slice(96 + 4 * f, 100 + 4 * f)
        for k in range(4):
            big[k, at, :] = nat[f, :, 128 * k : 128 * k + 128]
            big[4 + k, at, :] = nat[f, :, 3584 + 128 * k : 3712 + 128 * k]
            first = jnp.zeros((4, 128), f32)
            last = jnp.zeros((4, 128), f32)
            for t in range(8):
                v = nat[f, :, 128 * (8 * k + t) : 128 * (8 * k + t) + 128]
                first = first + roll(jnp.where(low, v, 0.0), 8 * t)
                last = last + roll(jnp.where(high, v, 0.0), 8 * t)
            big[8 + k, at, :] = first
            big[12 + k, at, :] = last
    for m in range(M):
        out[m] = big[m].astype(bf16)


def route_kernel(count, me, got, everyone, out, wide, sea, listed, numbers, collect, field, sem):
    for s in range(M):
        wide[s] = got[s].astype(f32)
    if count == M:
        listed[...] = wide[:, 132, :].astype(jnp.int32)
    else:
        listed[...] = everyone[...].astype(f32)[:, 4, :].astype(jnp.int32)
    copy = pltpu.make_async_copy(listed, numbers, sem)
    copy.start()
    me_now = me[0]
    m = lax.rem(me_now, M)
    first = me_now - m
    for s in range(M):
        for part in range(8):
            sea[s, part, 0:SEA, :] = wide[s, SEA * part : SEA * part + SEA, :]

    east = m < 4
    west = jnp.logical_and(m >= 4, m < 8)
    north = jnp.logical_and(m >= 8, m < 12)
    shift_c = jnp.where(east, 1, jnp.where(west, -1, 0))
    shift_r = jnp.where(north, 1, jnp.where(m >= 12, -1, 0))
    size = count * 4
    spread = jnp.broadcast_to(listed[...].astype(f32)[:, None, :], (count, 4, 128))
    spread = spread.reshape(size, 128)
    q_of = lax.broadcasted_iota(jnp.int32, (size, 128), 0) & 3
    lane_of = lanes((size, 128))
    column = jnp.sum(jnp.where(lane_of == q_of, spread, 0.0), axis=1, keepdims=True)
    row = jnp.sum(jnp.where(lane_of == q_of + 4, spread, 0.0), axis=1, keepdims=True)
    eye = lax.broadcasted_iota(jnp.int32, (size, size), 0) == lanes((size, size))
    number = jnp.sum(jnp.where(eye, column * 16.0 + row, 0.0), axis=0, keepdims=True)
    tc = column + shift_c.astype(f32)
    tc = jnp.where(tc < 0, tc + count, tc)
    tc = jnp.where(tc >= count, tc - count, tc)
    tr = row + shift_r.astype(f32)

    def one_hot(r):
        code = jnp.where((r >= 0) & (r < 16), tc * 16.0 + r, -1.0)
        return (code == number).astype(bf16)

    centre = one_hot(tr)
    before = one_hot(jnp.where(tr >= 0, tr - 1.0, -1.0))
    after = one_hot(jnp.where(tr < 16, tr + 1.0, 16.0))

    copy.wait()
    lane = lanes((8, 128))
    lane2 = lanes((1, 128))

    def cut(o, _):
        for q in range(4):
            c, r = numbers[o, q] - first, numbers[o, 4 + q]
            known = jnp.logical_and(c >= 0, c < M).astype(jnp.int32)
            c = jnp.clip(c, 0, M - 1)
            half, odd = r >> 1, r & 1
            near = half + 2 * odd - 1
            near_in = jnp.logical_and(near >= 0, near < 8).astype(jnp.int32)
            near = jnp.clip(near, 0, 7)
            a, b = sea[c, half, 0:8, :], sea[c, near, 0:8, :]
            inside = jnp.where(odd == 1, (lane >= 56).astype(jnp.int32), (lane < 72).astype(jnp.int32))
            edge = jnp.where(odd == 1, (lane < W).astype(jnp.int32), (lane >= 128 - W).astype(jnp.int32))
            value = jnp.where(inside * known == 1, a, jnp.where(edge * near_in * known == 1, b, 0.0))
            collect[o, pl.ds(q, 8, stride=4), :] = pltpu.roll(value, W + 64 * odd, 1)
            warm = sea[c, half, 8:12, :] * known.astype(f32)
            turn = pltpu.roll(warm, 64, 1)
            straight = jnp.where(odd == 1, turn, warm)
            crossed = jnp.where(odd == 1, warm, turn)
            for i in range(2):
                pair = jnp.where(lane2 < 64, straight[2 * i : 2 * i + 1], crossed[2 * i + 1 : 2 * i + 2])
                collect[o, 32 + 4 * i + q : 33 + 4 * i + q, :] = pair
        return 0

    lax.fori_loop(0, count, cut, 0, unroll=M)

    lane = lanes((size, 128))
    low, high = (lane & 63) < W, (lane & 63) >= BS - W
    rim = (m < 8).astype(f32)
    corners = []
    for jj in range(3):
        first_part = jnp.zeros((size, 128), f32)
        last_part = jnp.zeros((size, 128), f32)
        for i in range(min(4, NF - 4 * jj)):
            f = 4 * jj + i
            own = wide[:, 96 + 4 * f : 100 + 4 * f, :]
            if count > M:
                field[...] = jnp.zeros(field.shape, f32)
                field[pl.ds(first, M)] = own
                own = field[...]
            own = own.reshape(size, 128)
            if f in (2, 3):
                at = 16 * (f - 2)
                one = roll(collect[:, at : at + 4, :], -W).reshape(size, 128)
                two = roll(collect[:, at + 4 : at + 8, :], 64 - W).reshape(size, 128)
                own = own + rim * jnp.where(lane < 64, one, two)
            value = jnp.dot(centre, own.astype(bf16), preferred_element_type=f32)
            collect[:, 40 + 4 * f : 44 + 4 * f, :] = value.reshape(count, 4, 128)
            last_part = last_part + roll(jnp.where(high, own, 0.0), 16 * i)
            first_part = first_part + roll(jnp.where(low, own, 0.0), 16 * i)
        value = jnp.dot(before, last_part.astype(bf16), preferred_element_type=f32)
        value = value + jnp.dot(after, first_part.astype(bf16), preferred_element_type=f32)
        corners.append(value)
    for g in range(8):
        gap = jnp.zeros((size, 128), f32)
        for jj in range(3):
            start = 48 * g - 128 * jj
            if -48 < start < 128:
                place = lane + (start - FREE)
                there = (lane >= FREE) & (place >= 0) & (place < 128)
                gap = gap + jnp.where(there, roll(corners[jj], FREE - start), 0.0)
        at = slice(4 * g, 4 * g + 4)
        collect[:, at, :] = collect[:, at, :] + gap.reshape(count, 4, 128)
    for o in range(count):
        out[o] = collect[o].astype(bf16)


def ice_kernel(got, nat, conc, vol, motion, stress, grown, out, wide, ext, temp, flux):
    for m in range(M):
        wide[m] = got[m].astype(f32)
    lane = lanes((8, 128))

    def rim(m, j):
        return wide[m, 4 * j : 4 * j + 4, :]

    def two(a, b):
        return jnp.concatenate([a, b], axis=0)

    def natural(f, r):
        return two(
            nat[f, :, 128 * r : 128 * r + 128], nat[f, :, 128 * (r + 16) : 128 * (r + 16) + 128]
        )

    for f in range(11):
        ext[f, 0] = jnp.zeros((8, 128), f32)
        ext[f, 49] = jnp.zeros((8, 128), f32)
    lane4 = lanes((4, 128))
    corners = {}
    for m in range(8):
        for jj in range(3):
            value = jnp.zeros((4, 128), f32)
            for g in range(8):
                start = 48 * g - 128 * jj
                if -48 < start < 128:
                    there = (lane4 >= start) & (lane4 < start + 48)
                    value = jnp.where(there, roll(rim(m, g), start - FREE), value)
            corners[m, jj] = value
    inside = (lane >= W) & (lane < W + BS)
    for r in range(16):
        t = r % 8
        for p in range(2):
            own = (lane >> 3) == 8 * p + t
            for f in range(NF):
                north = two(rim(8 + r // 8, 10 + f), rim(10 + r // 8, 10 + f))
                south = two(rim(12 + r // 8, 10 + f), rim(14 + r // 8, 10 + f))
                sides = roll(jnp.where(own, north, south), -(56 + 64 * p + 8 * t))
                ext[f, 9 + 2 * r + p] = jnp.where(inside, roll(natural(f, r), 8 - 64 * p), sides)
    for f in range(NF):
        for y in range(8):
            p, i = y % 2, f % 4
            centre = two(rim(4 + y // 2, 10 + f), rim(y // 2, 10 + f))
            corner = two(corners[4 + y // 2, f // 4], corners[y // 2, f // 4])
            value = jnp.where(
                inside, roll(centre, 8 - 64 * p), roll(corner, -(56 + 64 * p + 16 * i))
            )
            ext[f, 1 + y] = two(value[0:4], ext[f, 33 + y, 0:4, :])
            ext[f, 41 + y] = two(ext[f, 9 + y, 4:8, :], value[4:8])
    where = {}
    for m in range(M):
        listed = [start + i for start, size in sea_rows(m) for i in range(size)]
        for k, row in enumerate(listed):
            where[row + W] = (m, k)
    blank = jnp.zeros((4, 128), f32)
    for y in range(48):
        for k in range(2):
            halves = [where.get(x) for x in (y, y + 32)]
            halves = [blank if at is None else rim(at[0], 4 * k + at[1]) for at in halves]
            value = two(*halves)
            ext[9 + k, 1 + y] = value
            ext[2 + k, 1 + y] = ext[2 + k, 1 + y] + value
    thick = ext[0, 1:49]
    ext[11, 1:49] = jnp.where(thick > 0.0, 1.0 / (thick + 1.0), 0.0)
    ext[1, 1:49] = jnp.where(thick > 0.0, 0.5 * ext[1, 1:49], 0.0)

    step = 8

    def speed(i, _):
        at = pl.ds(1 + i * step, step)
        full = pl.ds(i * step, step + 2)
        one, two_, shear = ext[6, full], ext[7, full], ext[8, full]
        add = one + two_
        sub = one[1:-1] - two_[1:-1]
        mid = shear[1:-1]
        fx = 0.25 * (add[2:] - add[:-2]) + 0.5 * (roll(mid, -1) - roll(mid, 1))
        fy = 0.5 * (shear[2:] - shear[:-2]) + 0.25 * (roll(sub, -1) - roll(sub, 1))
        thick, inverse = ext[0, at], ext[11, at]
        u, v = ext[4, at], ext[5, at]
        half = 0.5 * thick
        ext[4, at] = (thick * u + fx + ext[2, at] + half * v) * inverse
        ext[5, at] = (thick * v + fy + ext[3, at] - half * u) * inverse
        return 0

    def strain(i, _):
        at = pl.ds(1 + i * step, step)
        full = pl.ds(i * step, step + 2)
        uu, vv = ext[4, full], ext[5, full]
        u, v = uu[1:-1], vv[1:-1]
        ux = uu[2:] - uu[:-2]
        vx = vv[2:] - vv[:-2]
        uy = roll(u, -1) - roll(u, 1)
        vy = roll(v, -1) - roll(v, 1)
        divergence = 0.5 * (ux + vy)
        tension = 0.5 * (ux - vy)
        shearing = 0.5 * (uy + vx)
        inverse = lax.rsqrt(
            divergence * divergence + 0.25 * (tension * tension + shearing * shearing) + 0.01
        )
        half = jnp.where(ext[0, at] > 0.0, 0.5, 0.0)
        strong = ext[1, at]
        scaled = strong * inverse
        ext[6, at] = half * ext[6, at] + (scaled * divergence - strong)
        ext[7, at] = half * ext[7, at] + 0.25 * scaled * tension
        ext[8, at] = half * ext[8, at] + 0.125 * scaled * shearing
        return 0

    for _ in range(SUBCYCLES):
        for i in range(48 // step):
            speed(i, 0)
        for i in range(48 // step):
            strain(i, 0)

    def flat(f, r):
        a, b = ext[f, 9 + 2 * r], ext[f, 10 + 2 * r]
        return jnp.where(lane < 64, roll(a, -8), roll(b, 56))

    for r in range(32):
        temp[:, 128 * r : 128 * r + 128] = rim(r // 2, 8 + r % 2)
    for r in range(16):
        for f in range(3):
            value = flat(6 + f, r)
            stress[f, :, 128 * r : 128 * r + 128] = value[0:4]
            stress[f, :, 128 * (r + 16) : 128 * (r + 16) + 128] = value[4:8]
        cover, ice = natural(9, r), natural(0, r) > 0.0
        for f in range(2):
            value = flat(4 + f, r)
            motion[:, f, 128 * r : 128 * r + 128] = value[0:4]
            motion[:, f, 128 * (r + 16) : 128 * (r + 16) + 128] = value[4:8]
            tau = jnp.where(ice, cover * (value - flat(9 + f, r)), 0.0)
            at = 4 * ((f + 1) * 2 + r % 2)
            flux[r // 2, at : at + 4, :] = tau[0:4]
            flux[8 + r // 2, at : at + 4, :] = tau[4:8]
    step = 512
    for start in range(0, BS * BS, step):
        sl = pl.ds(start, step)
        excess = temp[:, sl] + 1.8
        half = jnp.where(nat[0, :, sl] > 0.0, 0.5, 0.0)
        heat = jnp.zeros((4, step), f32)
        for n in range(conc.shape[0]):
            volume = vol[n, :, sl]
            rate = half * conc[n, :, sl] * ((1.5 - 0.5 * n) - excess) / (1.0 + volume)
            later = jnp.maximum(volume + rate, 0.0)
            grown[n, :, sl] = later
            heat = heat + (later - volume)
        for k in range(step // 128):
            r = start // 128 + k
            at = 4 * (r % 2)
            flux[r // 2, at : at + 4, :] = heat[:, 128 * k : 128 * k + 128]
    for m in range(M):
        out[m] = flux[m].astype(bf16)


def return_kernel(count, got, codes, out, pick, wide):
    for s in range(M):
        wide[ROWS3 * s : ROWS3 * s + ROWS3, :] = got[s].astype(f32)
    column = lax.broadcasted_iota(jnp.int32, (ROWS4, M * ROWS3), 0)
    local_code = (column & 7) * 8 + (column >> 3)
    span = codes[0:1, :]

    def build(c, _):
        base = pl.multiple_of(c * ROWS4, ROWS4)
        pick[pl.ds(base, ROWS4), :] = (span == local_code + c * 64).astype(bf16)
        return 0

    lax.fori_loop(0, count, build, 0)
    value = jnp.dot(pick[...], wide[...].astype(bf16), preferred_element_type=f32)
    out[...] = value.astype(bf16).reshape(count, ROWS4, 128)


def ocean_kernel(temp, drift, wet, before, after, _, temp_out, drift_out):
    levels = temp.shape[0]
    shape = temp.shape[1:]
    lane = lanes(shape)
    row = lax.broadcasted_iota(jnp.int32, shape, 0)
    sea = wet[...].astype(f32)
    for k in range(levels + drift.shape[0]):
        mid = temp[k] if k < levels else drift[k - levels]
        east = jnp.where(row == shape[0] - 1, after[k], roll(mid, -1, 0))
        west = jnp.where(row == 0, before[k], roll(mid, 1, 0))
        north = jnp.where(lane == shape[1] - 1, 0.0, roll(mid, -1))
        south = jnp.where(lane == 0, 0.0, roll(mid, 1))
        change = 0.2 * (east + west + north + south - 4.0 * mid)
        if k < levels:
            vertical = jnp.zeros(shape, f32)
            if k + 1 < levels:
                vertical = vertical + (temp[k + 1] - mid)
            if k > 0:
                vertical = vertical - (mid - temp[k - 1])
            temp_out[k] = mid + sea * (change + 0.2 * vertical)
        else:
            drift_out[k - levels] = mid + sea * change


def final_kernel(
    rows, got, wet, temp, drift, temp_out, drift_out, wide, flux, held, arrive, leave
):
    arrivals = []
    for k in range(3):
        place = temp.at[0] if k == 0 else drift.at[k - 1]
        arrivals.append(pltpu.make_async_copy(place, held.at[k], arrive.at[k]))
        arrivals[-1].start()
    for m in range(M):
        wide[pl.ds(ROWS4 * m, ROWS4), :] = got[m].astype(f32)
    flux[0:16] = jnp.zeros((16,) + flux.shape[1:], f32)
    for slot in range(KMAX):
        r = rows[slot]
        for f in range(3):
            for h in range(2):
                value = wide[pl.ds(8 * (2 * f + h) + slot, M, stride=ROWS4), :]
                flux[r, pl.ds(BS * f + 2 * h, M, stride=4), :] = value
                flux[r, pl.ds(BS * f + 2 * h + 1, M, stride=4), :] = roll(value, 64)
    left = lanes((BS, 128)) < 64
    copies = []
    for k in range(3):
        arrivals[k].wait()
        for part in range(8):
            cut = slice(128 * part, 128 * part + 128)
            rows_of = slice(BS * k, BS * (k + 1))
            pair = jnp.where(left, flux[2 * part, rows_of, :], roll(flux[2 * part + 1, rows_of, :], 64))
            added = wet[:, cut].astype(f32) * pair
            held[k, :, cut] = held[k, :, cut] + added
        place = temp_out.at[0] if k == 0 else drift_out.at[k - 1]
        copies.append(pltpu.make_async_copy(held.at[k], place, leave.at[k]))
        copies[-1].start()
    for copy in copies:
        copy.wait()


def local(
    thermal_state,
    seawater_drift,
    sea_site_indicator,
    chosen_tile_numbers,
    chosen_floe_indicator,
    areal_fraction,
    thickness_amount,
    floe_motion,
    internal_traction,
    wind_traction,
):
    count = lax.axis_size("gx")
    groups = count // M
    me = lax.axis_index("gx")
    tiles = thermal_state.shape[2] // BS
    members = [[g * M + i for i in range(M)] for g in range(groups)]
    smem = pl.BlockSpec(memory_space=pltpu.SMEM)
    vmem = pl.BlockSpec(memory_space=pltpu.VMEM)
    depth, height = thermal_state.shape[1:]
    anywhere = pl.BlockSpec(memory_space=pl.ANY)
    top = pl.BlockSpec((1, depth, height), lambda i: (0, 0, 0))

    def whole(x):
        return pl.BlockSpec(x.shape, lambda i, n=len(x.shape): (0,) * n)

    def within(x):
        if groups == 1:
            return lax.all_to_all(x, "gx", 0, 0, tiled=True)
        return lax.all_to_all(x, "gx", 0, 0, axis_index_groups=members, tiled=True)

    def across(x):
        x = lax.all_to_all(x, "gx", 0, 0, tiled=True)
        if groups == 1:
            return x
        return jnp.sum(x.reshape((groups, M) + x.shape[1:]).astype(f32), 0).astype(bf16)

    tail = jnp.concatenate([thermal_state[:, depth - 1 :], seawater_drift[:, depth - 1 :]], 0)
    head = jnp.concatenate([thermal_state[:, :1], seawater_drift[:, :1]], 0)
    before = lax.ppermute(tail, "gx", [(i, (i + 1) % count) for i in range(count)])
    after = lax.ppermute(head, "gx", [((i + 1) % count, i) for i in range(count)])

    conc = jnp.transpose(areal_fraction, (1, 0, 2))
    vol = jnp.transpose(thickness_amount, (1, 0, 2))
    arrays = (
        thermal_state,
        seawater_drift,
        chosen_floe_indicator,
        conc,
        vol,
        floe_motion,
        jnp.transpose(internal_traction, (1, 0, 2)),
        wind_traction,
    )
    nat_shape = jax.ShapeDtypeStruct((10, 4, BS * BS), f32)
    one_shape = jax.ShapeDtypeStruct((M, ROWS1, 128), bf16)
    payload, nat = call(
        pack_kernel,
        (one_shape, nat_shape),
        scratch=(pltpu.VMEM((M, ROWS1, 128), f32),),
        grid=(1,),
        in_specs=[smem, top] + [whole(x) for x in arrays[1:]],
        out_specs=(whole(one_shape), whole(nat_shape)),
    )(chosen_tile_numbers, *arrays)
    got1 = within(payload)

    if groups == 1:
        everyone = got1
    else:
        mine = payload[0, 128:136]
        everyone = lax.all_gather(mine, "gx", axis=0, tiled=False)
    payload2 = call(
        functools.partial(route_kernel, count),
        pltpu.HBM((count, ROWS2, 128), bf16),
        scratch=(
            pltpu.VMEM((M, ROWS1, 128), f32),
            pltpu.VMEM((M, 8, 16, 128), f32),
            pltpu.VMEM((count, 128), jnp.int32),
            pltpu.SMEM((count, 128), jnp.int32),
            pltpu.VMEM((count, ROWS2, 128), f32),
            pltpu.VMEM((count, 4, 128), f32),
            pltpu.SemaphoreType.DMA,
        ),
        in_specs=[smem, vmem, vmem],
        out_specs=vmem,
        vmem=ROOM,
    )(me.reshape(1).astype(jnp.int32), got1, everyone)
    got2 = across(payload2)

    pairs = everyone[:, everyone.shape[1] - 4, 0:8].astype(jnp.int32)
    columns, rows = pairs[:, :4].reshape(-1), pairs[:, 4:].reshape(-1)
    ranks = jnp.sum(
        ((columns[None, :] == columns[:, None]) & (rows[None, :] < rows[:, None])).astype(jnp.int32), 1
    )
    slot = jnp.arange(KMAX, dtype=jnp.int32)
    mine = (columns[None, :] == me) & (ranks[None, :] == slot[:, None])
    slot_rows = 16 + jnp.sum(jnp.where(mine, rows[None, :] - 16, 0), 1)
    code = columns * 64 + ranks * 8
    code = lax.dynamic_slice_in_dim(code, (me // M) * (M * 4), M * 4, 0)
    item = jnp.arange(6, dtype=jnp.int32)
    codes = (code.reshape(M, 1, 4) + item[None, :, None]).reshape(1, M * ROWS3)

    motion, stress, grown, payload3 = call(
        ice_kernel,
        (
            jax.ShapeDtypeStruct(floe_motion.shape, f32),
            jax.ShapeDtypeStruct(arrays[6].shape, f32),
            jax.ShapeDtypeStruct(vol.shape, f32),
            pltpu.HBM((M, ROWS3, 128), bf16),
        ),
        scratch=(
            pltpu.VMEM((M, ROWS2, 128), f32),
            pltpu.VMEM((12, 50, 8, 128), f32),
            pltpu.VMEM((4, BS * BS), f32),
            pltpu.VMEM((M, ROWS3, 128), f32),
        ),
        in_specs=[vmem] * 4,
        out_specs=(vmem,) * 4,
        vmem=ROOM,
    )(got2, nat, conc, vol)
    stress = jnp.transpose(stress, (1, 0, 2))
    grown = jnp.transpose(grown, (1, 0, 2))
    temp_new, drift_new = call(
        ocean_kernel,
        (
            jax.ShapeDtypeStruct(thermal_state.shape, f32),
            jax.ShapeDtypeStruct(seawater_drift.shape, f32),
        ),
        in_specs=[vmem] * 5 + [anywhere],
        out_specs=(vmem, vmem),
        cost_estimate=pl.CostEstimate(flops=10**7, bytes_accessed=6 * 10**6, transcendentals=0),
    )(thermal_state, seawater_drift, sea_site_indicator, before, after, payload3)

    got3 = within(payload3)

    payload4 = call(
        functools.partial(return_kernel, count),
        pltpu.HBM((count, ROWS4, 128), bf16),
        scratch=(
            pltpu.VMEM((count * ROWS4, M * ROWS3), bf16),
            pltpu.VMEM((M * ROWS3, 128), f32),
        ),
        in_specs=[vmem, vmem],
        out_specs=vmem,
        vmem=ROOM,
    )(got3, codes)
    got4 = across(payload4)

    temp_later, drift_later = call(
        final_kernel,
        (
            jax.ShapeDtypeStruct(thermal_state.shape, f32),
            jax.ShapeDtypeStruct(seawater_drift.shape, f32),
        ),
        scratch=(
            pltpu.VMEM((M * ROWS4, 128), f32),
            pltpu.VMEM((17, 3 * BS, 128), f32),
            pltpu.VMEM((3, depth, height), f32),
            pltpu.SemaphoreType.DMA((3,)),
            pltpu.SemaphoreType.DMA((3,)),
        ),
        in_specs=[smem, vmem, vmem, anywhere, anywhere],
        out_specs=(anywhere, anywhere),
        input_output_aliases={3: 0, 4: 1},
        vmem=ROOM,
    )(slot_rows, got4, sea_site_indicator, temp_new, drift_new)
    return temp_later, drift_later, motion, stress, grown


def solution(mesh):
    return jax.shard_map(
        local,
        mesh=mesh,
        in_specs=(
            P("member", "gx", None),
            P("member", "gx", None),
            P("gx", None),
            P(("member", "gx")),
            P(("member", "gx"), None),
            P(("member", "gx"), None, None),
            P(("member", "gx"), None, None),
            P(("member", "gx"), None, None),
            P(("member", "gx"), None, None),
            P(("member", "gx"), None, None),
        ),
        out_specs=(
            P("member", "gx", None),
            P("member", "gx", None),
            P(("member", "gx"), None, None),
            P(("member", "gx"), None, None),
            P(("member", "gx"), None, None),
        ),
        check_vma=False,
    )
```

```python
import functools

import jax
import jax.numpy as jnp
from jax import lax
from jax.experimental import pallas as pl
from jax.experimental.pallas import tpu as pltpu
from jax.sharding import PartitionSpec as P

BS = 64
SUBCYCLES = 4
KMAX = 8
M = 16
W = 8
NF = 9
ROWS1 = 136
ROWS2 = 80
ROWS3 = 24
ROWS4 = 48
FREE = BS + 2 * W
SEA = 12
VMEM = 60 * 2**20
ROOM = 40 * 2**20
f32, bf16 = jnp.float32, jnp.bfloat16


def lanes(shape):
    return lax.broadcasted_iota(jnp.int32, shape, len(shape) - 1)


def roll(x, shift, axis=-1):
    axis = axis % x.ndim
    shift = shift % x.shape[axis]
    return x if shift == 0 else pltpu.roll(x, shift, axis)


def call(kernel, out_shape, scratch=(), in_specs=None, out_specs=None, vmem=VMEM, **kw):
    return pl.pallas_call(
        kernel,
        out_shape=out_shape,
        in_specs=in_specs,
        out_specs=out_specs,
        scratch_shapes=list(scratch),
        compiler_params=pltpu.CompilerParams(vmem_limit_bytes=vmem),
        **kw,
    )


def sea_rows(m):
    if m >= 8:
        return [(24 + 4 * (m - 8), 4)]
    return [(2 * m if m < 4 else 48 + 2 * m, 2), (8 + 2 * m, 2)]


def pack_kernel(ids, temp, drift, cells, conc, vol, motion, stress, wind, out, nat, big):
    tiles = temp.shape[2] // BS
    step = 512
    for start in range(0, BS * BS, step):
        sl = pl.ds(start, step)
        ice = cells[:, sl].astype(f32)
        cover = jnp.sum(conc[:, :, sl], axis=0)
        thick = jnp.sum(vol[:, :, sl], axis=0)
        nat[0, :, sl] = thick * ice
        nat[1, :, sl] = 2.0 * thick * jnp.exp(-5.0 * (1.0 - cover))
        nat[9, :, sl] = cover
        for k in range(2):
            nat[2 + k, :, sl] = wind[:, k, sl]
            nat[4 + k, :, sl] = motion[:, k, sl]
        for k in range(3):
            nat[6 + k, :, sl] = stress[k, :, sl]
    lane = lanes((4, 128))
    low, high = (lane & 63) < W, (lane & 63) >= BS - W
    lane_all = lanes((4, 128))
    row_all = lax.broadcasted_iota(jnp.int32, (4, 128), 0)
    listed = jnp.zeros((4, 128), f32)
    for q in range(4):
        number = ids[q]
        column, row = number // tiles, number % tiles
        listed = jnp.where(lane_all == q, column.astype(f32), listed)
        listed = jnp.where(lane_all == 4 + q, row.astype(f32), listed)
    listed = jnp.where(row_all == 0, listed, 0.0)
    for m in range(M):
        big[m, 132:136, :] = listed
        for part in range(8):
            cut = slice(128 * part, 128 * part + 128)
            at = SEA * part
            for k in range(2):
                place = at + 4 * k
                for start, size in sea_rows(m):
                    big[m, place : place + size, :] = drift[k, start : start + size, cut]
                    place += size
            big[m, at + 8 : at + 12, :] = temp[0, 4 * m : 4 * m + 4, cut]
    for f in range(NF):
        at = slice(96 + 4 * f, 100 + 4 * f)
        for k in range(4):
            big[k, at, :] = nat[f, :, 128 * k : 128 * k + 128]
            big[4 + k, at, :] = nat[f, :, 3584 + 128 * k : 3712 + 128 * k]
            first = jnp.zeros((4, 128), f32)
            last = jnp.zeros((4, 128), f32)
            for t in range(8):
                v = nat[f, :, 128 * (8 * k + t) : 128 * (8 * k + t) + 128]
                first = first + roll(jnp.where(low, v, 0.0), 8 * t)
                last = last + roll(jnp.where(high, v, 0.0), 8 * t)
            big[8 + k, at, :] = first
            big[12 + k, at, :] = last
    for m in range(M):
        out[m] = big[m].astype(bf16)


def route_kernel(count, me, got, everyone, out, wide, sea, listed, numbers, collect, field, sem):
    for s in range(M):
        wide[s] = got[s].astype(f32)
    if count == M:
        listed[...] = wide[:, 132, :].astype(jnp.int32)
    else:
        listed[...] = everyone[...].astype(f32)[:, 4, :].astype(jnp.int32)
    copy = pltpu.make_async_copy(listed, numbers, sem)
    copy.start()
    me_now = me[0]
    m = lax.rem(me_now, M)
    first = me_now - m
    for s in range(M):
        for part in range(8):
            sea[s, part, 0:SEA, :] = wide[s, SEA * part : SEA * part + SEA, :]

    east = m < 4
    west = jnp.logical_and(m >= 4, m < 8)
    north = jnp.logical_and(m >= 8, m < 12)
    shift_c = jnp.where(east, 1, jnp.where(west, -1, 0))
    shift_r = jnp.where(north, 1, jnp.where(m >= 12, -1, 0))
    size = count * 4
    spread = jnp.broadcast_to(listed[...].astype(f32)[:, None, :], (count, 4, 128))
    spread = spread.reshape(size, 128)
    q_of = lax.broadcasted_iota(jnp.int32, (size, 128), 0) & 3
    lane_of = lanes((size, 128))
    column = jnp.sum(jnp.where(lane_of == q_of, spread, 0.0), axis=1, keepdims=True)
    row = jnp.sum(jnp.where(lane_of == q_of + 4, spread, 0.0), axis=1, keepdims=True)
    eye = lax.broadcasted_iota(jnp.int32, (size, size), 0) == lanes((size, size))
    number = jnp.sum(jnp.where(eye, column * 16.0 + row, 0.0), axis=0, keepdims=True)
    tc = column + shift_c.astype(f32)
    tc = jnp.where(tc < 0, tc + count, tc)
    tc = jnp.where(tc >= count, tc - count, tc)
    tr = row + shift_r.astype(f32)

    def one_hot(r):
        code = jnp.where((r >= 0) & (r < 16), tc * 16.0 + r, -1.0)
        return (code == number).astype(bf16)

    centre = one_hot(tr)
    before = one_hot(jnp.where(tr >= 0, tr - 1.0, -1.0))
    after = one_hot(jnp.where(tr < 16, tr + 1.0, 16.0))

    copy.wait()
    lane = lanes((8, 128))
    lane2 = lanes((1, 128))

    def cut(o, _):
        for q in range(4):
            c, r = numbers[o, q] - first, numbers[o, 4 + q]
            known = jnp.logical_and(c >= 0, c < M).astype(jnp.int32)
            c = jnp.clip(c, 0, M - 1)
            half, odd = r >> 1, r & 1
            near = half + 2 * odd - 1
            near_in = jnp.logical_and(near >= 0, near < 8).astype(jnp.int32)
            near = jnp.clip(near, 0, 7)
            a, b = sea[c, half, 0:8, :], sea[c, near, 0:8, :]
            inside = jnp.where(odd == 1, (lane >= 56).astype(jnp.int32), (lane < 72).astype(jnp.int32))
            edge = jnp.where(odd == 1, (lane < W).astype(jnp.int32), (lane >= 128 - W).astype(jnp.int32))
            value = jnp.where(inside * known == 1, a, jnp.where(edge * near_in * known == 1, b, 0.0))
            collect[o, pl.ds(q, 8, stride=4), :] = pltpu.roll(value, W + 64 * odd, 1)
            warm = sea[c, half, 8:12, :] * known.astype(f32)
            turn = pltpu.roll(warm, 64, 1)
            straight = jnp.where(odd == 1, turn, warm)
            crossed = jnp.where(odd == 1, warm, turn)
            for i in range(2):
                pair = jnp.where(lane2 < 64, straight[2 * i : 2 * i + 1], crossed[2 * i + 1 : 2 * i + 2])
                collect[o, 32 + 4 * i + q : 33 + 4 * i + q, :] = pair
        return 0

    lax.fori_loop(0, count, cut, 0, unroll=M)

    lane = lanes((size, 128))
    low, high = (lane & 63) < W, (lane & 63) >= BS - W
    rim = (m < 8).astype(f32)
    corners = []
    for jj in range(3):
        first_part = jnp.zeros((size, 128), f32)
        last_part = jnp.zeros((size, 128), f32)
        for i in range(min(4, NF - 4 * jj)):
            f = 4 * jj + i
            own = wide[:, 96 + 4 * f : 100 + 4 * f, :]
            if count > M:
                field[...] = jnp.zeros(field.shape, f32)
                field[pl.ds(first, M)] = own
                own = field[...]
            own = own.reshape(size, 128)
            if f in (2, 3):
                at = 16 * (f - 2)
                one = roll(collect[:, at : at + 4, :], -W).reshape(size, 128)
                two = roll(collect[:, at + 4 : at + 8, :], 64 - W).reshape(size, 128)
                own = own + rim * jnp.where(lane < 64, one, two)
            value = jnp.dot(centre, own.astype(bf16), preferred_element_type=f32)
            collect[:, 40 + 4 * f : 44 + 4 * f, :] = value.reshape(count, 4, 128)
            last_part = last_part + roll(jnp.where(high, own, 0.0), 16 * i)
            first_part = first_part + roll(jnp.where(low, own, 0.0), 16 * i)
        value = jnp.dot(before, last_part.astype(bf16), preferred_element_type=f32)
        value = value + jnp.dot(after, first_part.astype(bf16), preferred_element_type=f32)
        corners.append(value)
    for g in range(8):
        gap = jnp.zeros((size, 128), f32)
        for jj in range(3):
            start = 48 * g - 128 * jj
            if -48 < start < 128:
                place = lane + (start - FREE)
                there = (lane >= FREE) & (place >= 0) & (place < 128)
                gap = gap + jnp.where(there, roll(corners[jj], FREE - start), 0.0)
        at = slice(4 * g, 4 * g + 4)
        collect[:, at, :] = collect[:, at, :] + gap.reshape(count, 4, 128)
    for o in range(count):
        out[o] = collect[o].astype(bf16)


def ice_kernel(got, nat, conc, vol, motion, stress, grown, out, wide, ext, temp, flux):
    for m in range(M):
        wide[m] = got[m].astype(f32)
    lane = lanes((8, 128))

    def rim(m, j):
        return wide[m, 4 * j : 4 * j + 4, :]

    def two(a, b):
        return jnp.concatenate([a, b], axis=0)

    def natural(f, r):
        return two(
            nat[f, :, 128 * r : 128 * r + 128], nat[f, :, 128 * (r + 16) : 128 * (r + 16) + 128]
        )

    for f in range(11):
        ext[f, 0] = jnp.zeros((8, 128), f32)
        ext[f, 49] = jnp.zeros((8, 128), f32)
    lane4 = lanes((4, 128))
    corners = {}
    for m in range(8):
        for jj in range(3):
            value = jnp.zeros((4, 128), f32)
            for g in range(8):
                start = 48 * g - 128 * jj
                if -48 < start < 128:
                    there = (lane4 >= start) & (lane4 < start + 48)
                    value = jnp.where(there, roll(rim(m, g), start - FREE), value)
            corners[m, jj] = value
    inside = (lane >= W) & (lane < W + BS)
    for r in range(16):
        t = r % 8
        for p in range(2):
            own = (lane >> 3) == 8 * p + t
            for f in range(NF):
                north = two(rim(8 + r // 8, 10 + f), rim(10 + r // 8, 10 + f))
                south = two(rim(12 + r // 8, 10 + f), rim(14 + r // 8, 10 + f))
                sides = roll(jnp.where(own, north, south), -(56 + 64 * p + 8 * t))
                ext[f, 9 + 2 * r + p] = jnp.where(inside, roll(natural(f, r), 8 - 64 * p), sides)
    for f in range(NF):
        for y in range(8):
            p, i = y % 2, f % 4
            centre = two(rim(4 + y // 2, 10 + f), rim(y // 2, 10 + f))
            corner = two(corners[4 + y // 2, f // 4], corners[y // 2, f // 4])
            value = jnp.where(
                inside, roll(centre, 8 - 64 * p), roll(corner, -(56 + 64 * p + 16 * i))
            )
            ext[f, 1 + y] = two(value[0:4], ext[f, 33 + y, 0:4, :])
            ext[f, 41 + y] = two(ext[f, 9 + y, 4:8, :], value[4:8])
    where = {}
    for m in range(M):
        listed = [start + i for start, size in sea_rows(m) for i in range(size)]
        for k, row in enumerate(listed):
            where[row + W] = (m, k)
    blank = jnp.zeros((4, 128), f32)
    for y in range(48):
        for k in range(2):
            halves = [where.get(x) for x in (y, y + 32)]
            halves = [blank if at is None else rim(at[0], 4 * k + at[1]) for at in halves]
            value = two(*halves)
            ext[9 + k, 1 + y] = value
            ext[2 + k, 1 + y] = ext[2 + k, 1 + y] + value
    thick = ext[0, 1:49]
    ext[11, 1:49] = jnp.where(thick > 0.0, 1.0 / (thick + 1.0), 0.0)
    ext[1, 1:49] = jnp.where(thick > 0.0, 0.5 * ext[1, 1:49], 0.0)

    step = 8

    def speed(i, _):
        at = pl.ds(1 + i * step, step)
        full = pl.ds(i * step, step + 2)
        one, two_, shear = ext[6, full], ext[7, full], ext[8, full]
        add = one + two_
        sub = one[1:-1] - two_[1:-1]
        mid = shear[1:-1]
        fx = 0.25 * (add[2:] - add[:-2]) + 0.5 * (roll(mid, -1) - roll(mid, 1))
        fy = 0.5 * (shear[2:] - shear[:-2]) + 0.25 * (roll(sub, -1) - roll(sub, 1))
        thick, inverse = ext[0, at], ext[11, at]
        u, v = ext[4, at], ext[5, at]
        half = 0.5 * thick
        ext[4, at] = (thick * u + fx + ext[2, at] + half * v) * inverse
        ext[5, at] = (thick * v + fy + ext[3, at] - half * u) * inverse
        return 0

    def strain(i, _):
        at = pl.ds(1 + i * step, step)
        full = pl.ds(i * step, step + 2)
        uu, vv = ext[4, full], ext[5, full]
        u, v = uu[1:-1], vv[1:-1]
        ux = uu[2:] - uu[:-2]
        vx = vv[2:] - vv[:-2]
        uy = roll(u, -1) - roll(u, 1)
        vy = roll(v, -1) - roll(v, 1)
        divergence = 0.5 * (ux + vy)
        tension = 0.5 * (ux - vy)
        shearing = 0.5 * (uy + vx)
        inverse = lax.rsqrt(
            divergence * divergence + 0.25 * (tension * tension + shearing * shearing) + 0.01
        )
        half = jnp.where(ext[0, at] > 0.0, 0.5, 0.0)
        strong = ext[1, at]
        scaled = strong * inverse
        ext[6, at] = half * ext[6, at] + (scaled * divergence - strong)
        ext[7, at] = half * ext[7, at] + 0.25 * scaled * tension
        ext[8, at] = half * ext[8, at] + 0.125 * scaled * shearing
        return 0

    for _ in range(SUBCYCLES):
        for i in range(48 // step):
            speed(i, 0)
        for i in range(48 // step):
            strain(i, 0)

    def flat(f, r):
        a, b = ext[f, 9 + 2 * r], ext[f, 10 + 2 * r]
        return jnp.where(lane < 64, roll(a, -8), roll(b, 56))

    for r in range(32):
        temp[:, 128 * r : 128 * r + 128] = rim(r // 2, 8 + r % 2)
    for r in range(16):
        for f in range(3):
            value = flat(6 + f, r)
            stress[f, :, 128 * r : 128 * r + 128] = value[0:4]
            stress[f, :, 128 * (r + 16) : 128 * (r + 16) + 128] = value[4:8]
        cover, ice = natural(9, r), natural(0, r) > 0.0
        for f in range(2):
            value = flat(4 + f, r)
            motion[:, f, 128 * r : 128 * r + 128] = value[0:4]
            motion[:, f, 128 * (r + 16) : 128 * (r + 16) + 128] = value[4:8]
            tau = jnp.where(ice, cover * (value - flat(9 + f, r)), 0.0)
            at = 4 * ((f + 1) * 2 + r % 2)
            flux[r // 2, at : at + 4, :] = tau[0:4]
            flux[8 + r // 2, at : at + 4, :] = tau[4:8]
    step = 512
    for start in range(0, BS * BS, step):
        sl = pl.ds(start, step)
        excess = temp[:, sl] + 1.8
        half = jnp.where(nat[0, :, sl] > 0.0, 0.5, 0.0)
        heat = jnp.zeros((4, step), f32)
        for n in range(conc.shape[0]):
            volume = vol[n, :, sl]
            rate = half * conc[n, :, sl] * ((1.5 - 0.5 * n) - excess) / (1.0 + volume)
            later = jnp.maximum(volume + rate, 0.0)
            grown[n, :, sl] = later
            heat = heat + (later - volume)
        for k in range(step // 128):
            r = start // 128 + k
            at = 4 * (r % 2)
            flux[r // 2, at : at + 4, :] = heat[:, 128 * k : 128 * k + 128]
    for m in range(M):
        out[m] = flux[m].astype(bf16)


def return_kernel(count, got, codes, out, pick, wide):
    for s in range(M):
        wide[ROWS3 * s : ROWS3 * s + ROWS3, :] = got[s].astype(f32)
    column = lax.broadcasted_iota(jnp.int32, (ROWS4, M * ROWS3), 0)
    local_code = (column & 7) * 8 + (column >> 3)
    span = codes[0:1, :]

    def build(c, _):
        base = pl.multiple_of(c * ROWS4, ROWS4)
        pick[pl.ds(base, ROWS4), :] = (span == local_code + c * 64).astype(bf16)
        return 0

    lax.fori_loop(0, count, build, 0)
    value = jnp.dot(pick[...], wide[...].astype(bf16), preferred_element_type=f32)
    out[...] = value.astype(bf16).reshape(count, ROWS4, 128)


def ocean_kernel(temp, drift, wet, before, after, _, temp_out, drift_out):
    levels = temp.shape[0]
    shape = temp.shape[1:]
    lane = lanes(shape)
    row = lax.broadcasted_iota(jnp.int32, shape, 0)
    sea = wet[...].astype(f32)
    for k in range(levels + drift.shape[0]):
        mid = temp[k] if k < levels else drift[k - levels]
        east = jnp.where(row == shape[0] - 1, after[k], roll(mid, -1, 0))
        west = jnp.where(row == 0, before[k], roll(mid, 1, 0))
        north = jnp.where(lane == shape[1] - 1, 0.0, roll(mid, -1))
        south = jnp.where(lane == 0, 0.0, roll(mid, 1))
        change = 0.2 * (east + west + north + south - 4.0 * mid)
        if k < levels:
            vertical = jnp.zeros(shape, f32)
            if k + 1 < levels:
                vertical = vertical + (temp[k + 1] - mid)
            if k > 0:
                vertical = vertical - (mid - temp[k - 1])
            temp_out[k] = mid + sea * (change + 0.2 * vertical)
        else:
            drift_out[k - levels] = mid + sea * change


def final_kernel(rows, got, wet, temp, drift, temp_out, drift_out, wide, flux):
    for m in range(M):
        wide[pl.ds(ROWS4 * m, ROWS4), :] = got[m].astype(f32)
    flux[0:16] = jnp.zeros((16,) + flux.shape[1:], f32)
    for slot in range(KMAX):
        r = rows[slot]
        for f in range(3):
            for h in range(2):
                value = wide[pl.ds(8 * (2 * f + h) + slot, M, stride=ROWS4), :]
                flux[r, pl.ds(BS * f + 2 * h, M, stride=4), :] = value
                flux[r, pl.ds(BS * f + 2 * h + 1, M, stride=4), :] = roll(value, 64)
    left = lanes((BS, 128)) < 64
    for k in range(3):
        for part in range(8):
            cut = slice(128 * part, 128 * part + 128)
            rows_of = slice(BS * k, BS * (k + 1))
            pair = jnp.where(left, flux[2 * part, rows_of, :], roll(flux[2 * part + 1, rows_of, :], 64))
            added = wet[:, cut].astype(f32) * pair
            if k == 0:
                temp_out[0, :, cut] = temp[0, :, cut] + added
            else:
                drift_out[k - 1, :, cut] = drift[k - 1, :, cut] + added


def local(
    thermal_state,
    seawater_drift,
    sea_site_indicator,
    chosen_tile_numbers,
    chosen_floe_indicator,
    areal_fraction,
    thickness_amount,
    floe_motion,
    internal_traction,
    wind_traction,
):
    count = lax.axis_size("gx")
    groups = count // M
    me = lax.axis_index("gx")
    tiles = thermal_state.shape[2] // BS
    members = [[g * M + i for i in range(M)] for g in range(groups)]
    smem = pl.BlockSpec(memory_space=pltpu.SMEM)
    vmem = pl.BlockSpec(memory_space=pltpu.VMEM)
    depth, height = thermal_state.shape[1:]
    anywhere = pl.BlockSpec(memory_space=pl.ANY)
    top = pl.BlockSpec((1, depth, height), lambda i: (0, 0, 0))

    def whole(x):
        return pl.BlockSpec(x.shape, lambda i, n=len(x.shape): (0,) * n)

    def within(x):
        if groups == 1:
            return lax.all_to_all(x, "gx", 0, 0, tiled=True)
        return lax.all_to_all(x, "gx", 0, 0, axis_index_groups=members, tiled=True)

    def across(x):
        x = lax.all_to_all(x, "gx", 0, 0, tiled=True)
        if groups == 1:
            return x
        return jnp.sum(x.reshape((groups, M) + x.shape[1:]).astype(f32), 0).astype(bf16)

    tail = jnp.concatenate([thermal_state[:, depth - 1 :], seawater_drift[:, depth - 1 :]], 0)
    head = jnp.concatenate([thermal_state[:, :1], seawater_drift[:, :1]], 0)
    before = lax.ppermute(tail, "gx", [(i, (i + 1) % count) for i in range(count)])
    after = lax.ppermute(head, "gx", [((i + 1) % count, i) for i in range(count)])

    conc = jnp.transpose(areal_fraction, (1, 0, 2))
    vol = jnp.transpose(thickness_amount, (1, 0, 2))
    arrays = (
        thermal_state,
        seawater_drift,
        chosen_floe_indicator,
        conc,
        vol,
        floe_motion,
        jnp.transpose(internal_traction, (1, 0, 2)),
        wind_traction,
    )
    nat_shape = jax.ShapeDtypeStruct((10, 4, BS * BS), f32)
    one_shape = jax.ShapeDtypeStruct((M, ROWS1, 128), bf16)
    payload, nat = call(
        pack_kernel,
        (one_shape, nat_shape),
        scratch=(pltpu.VMEM((M, ROWS1, 128), f32),),
        grid=(1,),
        in_specs=[smem, top] + [whole(x) for x in arrays[1:]],
        out_specs=(whole(one_shape), whole(nat_shape)),
    )(chosen_tile_numbers, *arrays)
    got1 = within(payload)

    if groups == 1:
        everyone = got1
    else:
        mine = payload[0, 128:136]
        everyone = lax.all_gather(mine, "gx", axis=0, tiled=False)
    payload2 = call(
        functools.partial(route_kernel, count),
        pltpu.HBM((count, ROWS2, 128), bf16),
        scratch=(
            pltpu.VMEM((M, ROWS1, 128), f32),
            pltpu.VMEM((M, 8, 16, 128), f32),
            pltpu.VMEM((count, 128), jnp.int32),
            pltpu.SMEM((count, 128), jnp.int32),
            pltpu.VMEM((count, ROWS2, 128), f32),
            pltpu.VMEM((count, 4, 128), f32),
            pltpu.SemaphoreType.DMA,
        ),
        in_specs=[smem, vmem, vmem],
        out_specs=vmem,
        vmem=ROOM,
    )(me.reshape(1).astype(jnp.int32), got1, everyone)
    got2 = across(payload2)

    pairs = everyone[:, everyone.shape[1] - 4, 0:8].astype(jnp.int32)
    columns, rows = pairs[:, :4].reshape(-1), pairs[:, 4:].reshape(-1)
    ranks = jnp.sum(
        ((columns[None, :] == columns[:, None]) & (rows[None, :] < rows[:, None])).astype(jnp.int32), 1
    )
    slot = jnp.arange(KMAX, dtype=jnp.int32)
    mine = (columns[None, :] == me) & (ranks[None, :] == slot[:, None])
    slot_rows = 16 + jnp.sum(jnp.where(mine, rows[None, :] - 16, 0), 1)
    code = columns * 64 + ranks * 8
    code = lax.dynamic_slice_in_dim(code, (me // M) * (M * 4), M * 4, 0)
    item = jnp.arange(6, dtype=jnp.int32)
    codes = (code.reshape(M, 1, 4) + item[None, :, None]).reshape(1, M * ROWS3)

    motion, stress, grown, payload3 = call(
        ice_kernel,
        (
            jax.ShapeDtypeStruct(floe_motion.shape, f32),
            jax.ShapeDtypeStruct(arrays[6].shape, f32),
            jax.ShapeDtypeStruct(vol.shape, f32),
            pltpu.HBM((M, ROWS3, 128), bf16),
        ),
        scratch=(
            pltpu.VMEM((M, ROWS2, 128), f32),
            pltpu.VMEM((12, 50, 8, 128), f32),
            pltpu.VMEM((4, BS * BS), f32),
            pltpu.VMEM((M, ROWS3, 128), f32),
        ),
        in_specs=[vmem] * 4,
        out_specs=(vmem,) * 4,
        vmem=ROOM,
    )(got2, nat, conc, vol)
    stress = jnp.transpose(stress, (1, 0, 2))
    grown = jnp.transpose(grown, (1, 0, 2))
    temp_new, drift_new = call(
        ocean_kernel,
        (
            jax.ShapeDtypeStruct(thermal_state.shape, f32),
            jax.ShapeDtypeStruct(seawater_drift.shape, f32),
        ),
        in_specs=[vmem] * 5 + [anywhere],
        out_specs=(vmem, vmem),
        cost_estimate=pl.CostEstimate(flops=10**7, bytes_accessed=6 * 10**6, transcendentals=0),
    )(thermal_state, seawater_drift, sea_site_indicator, before, after, payload3)

    got3 = within(payload3)

    payload4 = call(
        functools.partial(return_kernel, count),
        pltpu.HBM((count, ROWS4, 128), bf16),
        scratch=(
            pltpu.VMEM((count * ROWS4, M * ROWS3), bf16),
            pltpu.VMEM((M * ROWS3, 128), f32),
        ),
        in_specs=[vmem, vmem],
        out_specs=vmem,
        vmem=ROOM,
    )(got3, codes)
    got4 = across(payload4)

    temp_later, drift_later = call(
        final_kernel,
        (
            jax.ShapeDtypeStruct(thermal_state.shape, f32),
            jax.ShapeDtypeStruct(seawater_drift.shape, f32),
        ),
        scratch=(
            pltpu.VMEM((M * ROWS4, 128), f32),
            pltpu.VMEM((17, 3 * BS, 128), f32),
        ),
        grid=(1,),
        in_specs=[smem, whole(got4), whole(sea_site_indicator), top, whole(drift_new)],
        out_specs=(top, whole(drift_new)),
        input_output_aliases={3: 0, 4: 1},
        vmem=ROOM,
    )(slot_rows, got4, sea_site_indicator, temp_new, drift_new)
    return temp_later, drift_later, motion, stress, grown


def solution(mesh):
    return jax.shard_map(
        local,
        mesh=mesh,
        in_specs=(
            P("member", "gx", None),
            P("member", "gx", None),
            P("gx", None),
            P(("member", "gx")),
            P(("member", "gx"), None),
            P(("member", "gx"), None, None),
            P(("member", "gx"), None, None),
            P(("member", "gx"), None, None),
            P(("member", "gx"), None, None),
            P(("member", "gx"), None, None),
        ),
        out_specs=(
            P("member", "gx", None),
            P("member", "gx", None),
            P(("member", "gx"), None, None),
            P(("member", "gx"), None, None),
            P(("member", "gx"), None, None),
        ),
        check_vma=False,
    )
```
